256 devices in a mesh: fsdp: 16 (over x, y_lo, core), tensor: 16 (over y_hi, z).
Axes of the slice: x: 4, y: 4 (y_hi: 2, y_lo: 2; y = y_hi * 2 + y_lo), z: 8, core: 2. Of those that a mesh axis runs over, the one named last changes fastest.
Arguments:
- queries: bfloat16 [8192, 6144], P('fsdp', 'tensor'), may hold values from -6 to 6
- keys: bfloat16 [8192, 6144], P('fsdp', 'tensor'), may hold values from -12 to 12
- values: bfloat16 [8192, 6144], P('fsdp', 'tensor'), may hold values from -6 to 6
- grad_out: bfloat16 [8192, 6144], P('fsdp', 'tensor'), may hold values from -6 to 6
- out_weight: bfloat16 [6144, 6144], P('fsdp', 'tensor'), may hold values from -0.078125 to 0.078125
Outputs:
- d_queries: bfloat16 [8192, 6144], P('fsdp', 'tensor')
- d_keys: bfloat16 [8192, 6144], P('fsdp', 'tensor')
- d_values: bfloat16 [8192, 6144], P('fsdp', 'tensor')
- d_weight: float32 [6144, 6144], P('fsdp', 'tensor')
The draws below stay inside these ranges and needn't reach their ends.
All inputs are finite; a program needn't handle non-finite values.
Results may differ from the reference program's by a relative error of at most 0.0079.
Values may be sent and summed in bfloat16 or wider, within the bound.
A program may use at most 128 MiB of HBM per device.

```python
import jax
import jax.numpy as jnp
from jax import lax

D = 6144
HEADS = 48
HEAD_DIM = 128
SEQ = 512
INNER = 6144
TOKENS = 8192
N_FSDP = 16


def draw_queries(key, part):
    key = jax.random.fold_in(key, 1)
    drawn_values = jnp.clip(jax.random.normal(key, (TOKENS, INNER), jnp.float32), -6.0, 6.0)
    return drawn_values.astype(jnp.bfloat16)


def draw_keys(key, part):
    key = jax.random.fold_in(key, 2)
    drawn_values = 2.0 * jnp.clip(jax.random.normal(key, (TOKENS, INNER), jnp.float32), -6.0, 6.0)
    return drawn_values.astype(jnp.bfloat16)


def spiked(drawn, key, source, target, blocks, factor):
    owner, partner = [(jnp.arange(drawn.shape[axis_at]) // (drawn.shape[axis_at] // blocks)).reshape([-1 if axis == axis_at else 1 for axis in range(drawn.ndim)]) for axis_at in (source, target)]
    chosen = jax.random.permutation(key, blocks)[partner]
    strong = (owner == chosen) | (owner == (partner + blocks // 2) % blocks)
    return jnp.where(strong, factor * drawn, drawn)


def block_scale(own_key, extent, cuts, smallest, largest):
    def one(dim, shards_of):
        heights = jax.random.uniform(jax.random.fold_in(jax.random.fold_in(own_key, 6), dim), (shards_of,), jnp.float32, smallest / len(cuts), largest / len(cuts))
        return jnp.repeat(jnp.exp(heights), extent[dim] // shards_of).reshape((-1,) + (1,) * (len(extent) - dim - 1))

    loudness = one(*cuts[0])
    for cut in cuts[1:]:
        loudness = loudness * one(*cut)
    return loudness


def normal_values(own_key, dims, scale, bound, cuts=(), held_as=jnp.bfloat16):
    values = scale * jax.random.normal(own_key, dims, jnp.float32)
    if cuts:
        values = values * block_scale(own_key, dims, cuts, -0.22, 0.18)
    return jnp.clip(values, -bound, bound).astype(held_as)


def noise_with(own_key, dims, width, most, pieces, heavy, kind=jnp.bfloat16):
    array = width * jax.random.normal(own_key, dims, jnp.float32)
    if pieces:
        array = array * block_scale(own_key, dims, pieces, -0.22, 0.18)
    return jnp.clip(spiked(array, jax.random.fold_in(own_key, 3), *heavy), -most, most).astype(kind)


def setup_inputs(seed: int = 0) -> dict:
    streams_of = jax.random.split(jax.random.key(seed), 6)
    return {
        "queries": draw_queries(jax.random.fold_in(streams_of[5], 71), 0),
        "keys": draw_keys(jax.random.fold_in(streams_of[5], 71), 0),
        "values": normal_values(streams_of[2], (TOKENS, INNER), 1.0, 6.0, ((0, 16), (1, 16))),
        "grad_out": noise_with(streams_of[3], (TOKENS, D), 1.0, 6.0, ((0, 16), (1, 16)), (0, 1, 16, 2.0)),
        "out_weight": normal_values(streams_of[4], (D, INNER), INNER ** -0.5, 0.078125, ((0, 16), (1, 16))),
    }


def head_gradients(operands):
    query_rows, key_rows, value_rows, grad_rows = operands
    score_scale = HEAD_DIM ** -0.5
    scores = jnp.dot(query_rows, key_rows.T, preferred_element_type=jnp.float32) * score_scale
    row_max = jnp.max(scores, axis=-1, keepdims=True)
    exponent = jnp.exp(scores - row_max)
    probs = exponent / jnp.sum(exponent, axis=-1, keepdims=True)
    prob_rounded = probs.astype(jnp.bfloat16)
    attended = jnp.dot(prob_rounded, value_rows, preferred_element_type=jnp.float32).astype(jnp.bfloat16)
    grad_probs = jnp.dot(grad_rows, value_rows.T, preferred_element_type=jnp.float32)
    row_dot = jnp.sum(probs * grad_probs, axis=-1, keepdims=True)
    grad_scores = (probs * (grad_probs - row_dot) * score_scale).astype(jnp.bfloat16)
    d_query = jnp.dot(grad_scores, key_rows, preferred_element_type=jnp.float32).astype(jnp.bfloat16)
    d_key = jnp.dot(grad_scores.T, query_rows, preferred_element_type=jnp.float32).astype(jnp.bfloat16)
    d_value = jnp.dot(prob_rounded.T, grad_rows, preferred_element_type=jnp.float32).astype(jnp.bfloat16)
    return attended, d_query, d_key, d_value


def split_heads(matrix):
    shaped = matrix.reshape(N_FSDP, SEQ, HEADS, HEAD_DIM).transpose(0, 2, 1, 3)
    return shaped.reshape(N_FSDP * HEADS, SEQ, HEAD_DIM)


def join_heads(stacked):
    shaped = stacked.reshape(N_FSDP, HEADS, SEQ, HEAD_DIM).transpose(0, 2, 1, 3)
    return shaped.reshape(TOKENS, INNER)


def reference(queries, keys, values, grad_out, out_weight):
    d_attended = jnp.dot(grad_out, out_weight, preferred_element_type=jnp.float32).astype(jnp.bfloat16)
    attended, d_query, d_key, d_value = lax.map(
        head_gradients,
        (split_heads(queries), split_heads(keys), split_heads(values), split_heads(d_attended)))
    d_weight = jnp.dot(grad_out.T, join_heads(attended), preferred_element_type=jnp.float32)
    return join_heads(d_query), join_heads(d_key), join_heads(d_value), d_weight
```

```python
import functools

import jax
import jax.numpy as jnp
from jax import lax
from jax.experimental import pallas as pl
from jax.experimental.pallas import tpu as pltpu
from jax.sharding import PartitionSpec as P

HEAD_DIM = 128
SCALE = HEAD_DIM ** (-0.5)
MESH = pl.DeviceIdType.MESH
BF = jnp.bfloat16
F32 = jnp.float32
TN = (((0,), (0,)), ((), ()))
NT = (((1,), (1,)), ((), ()))

SEQ = 512
WIDTH = 384
HALF = 192
HEADS = 3
QCHUNK = 256


def dot(a, b):
    return jnp.dot(a, b, preferred_element_type=F32)


def dotg(a, b, dims):
    return lax.dot_general(a, b, dims, preferred_element_type=F32)


def kernel(
    q_ref, k_ref, v_ref, g_ref, w_ref,
    dq_ref, dk_ref, dv_ref, dw_ref,
    at, ag, wg, t2, probs, cacc, csend, crecv, gbuf, dall, dr, xr, fs, yr, fkeep,
    z_s, z_r, a_s, a_r, wp_s, wp_r, wy_s, wy_r, wx_s, wx_r, wc_s, wc_r,
    t_s, t_r, c_s, c_r, dc_s, dc_r, dx_s, dx_r, dy_s, dy_r,
):
    f = lax.axis_index("fsdp")
    t = lax.axis_index("tensor")
    x = lax.div(f, 4)
    yl = lax.rem(lax.div(f, 2), 2)
    c = lax.rem(f, 2)
    h = lax.div(t, 8)
    z = lax.rem(t, 8)
    oh = 1 - h
    oyl = 1 - yl
    oc = 1 - c

    def dev(x_=None, yl_=None, c_=None, h_=None, z_=None):
        x_ = x if x_ is None else x_
        yl_ = yl if yl_ is None else yl_
        c_ = c if c_ is None else c_
        h_ = h if h_ is None else h_
        z_ = z if z_ is None else z_
        return (x_ * 4 + yl_ * 2 + c_, h_ * 8 + z_)

    def zoff(d):
        return lax.rem(z + 8 + d, 8)

    def xoff(d):
        return lax.rem(x + 4 + d, 4)

    def rcopy(src, dst, ssem, rsem, device):
        return pltpu.make_async_remote_copy(
            src_ref=src, dst_ref=dst, send_sem=ssem, recv_sem=rsem,
            device_id=device, device_id_type=MESH,
        )

    peers = [
        dev(z_=zoff(1)), dev(z_=zoff(-1)),
        dev(h_=oh), dev(yl_=oyl), dev(yl_=oyl, h_=oh),
        dev(x_=xoff(1)), dev(x_=xoff(-1)), dev(x_=xoff(2)),
        dev(c_=oc),
    ]
    barrier = pltpu.get_barrier_semaphore()
    for peer in peers:
        pl.semaphore_signal(barrier, inc=1, device_id=peer, device_id_type=MESH)
    pl.semaphore_wait(barrier, len(peers))

    sent = []

    def zcopy(way, k, own):
        src = zoff(-k) if way == 0 else zoff(k)
        piece = h if own else oh
        to = dev(z_=zoff(1)) if way == 0 else dev(z_=zoff(-1))
        i = 2 * k + (0 if own else 1)
        ref = ag.at[src, piece]
        return rcopy(ref, ref, z_s.at[way, i], z_r.at[way, i], to)

    def wblock(x_, yl_, c_=None):
        c_ = c if c_ is None else c_
        return wg.at[lax.rem(x_, 2) * 4 + yl_ * 2 + c_, lax.div(x_, 2)]

    def wycopy():
        ref = wblock(x, yl)
        return rcopy(ref, ref, wy_s.at[0], wy_r.at[0], dev(yl_=oyl))

    def wxcopy(way, i):
        to = dev(x_=xoff(1)) if way == 0 else dev(x_=xoff(-1))
        if i == 0:
            ref = wblock(x, yl)
        elif i == 1:
            ref = wblock(x, oyl)
        else:
            ref = wblock(xoff(-1), yl) if way == 0 else wblock(xoff(1), oyl)
        return rcopy(ref, ref, wx_s.at[way, i], wx_r.at[way, i], to)

    def wccopy(d, own_row):
        ref = wblock(xoff(d), yl if own_row else oyl)
        i = 2 * d + (0 if own_row else 1)
        return rcopy(ref, ref, wc_s.at[i], wc_r.at[i], dev(c_=oc))

    def tcopy(n):
        return rcopy(
            t2.at[:, pl.ds(n * HEAD_DIM, HEAD_DIM)],
            t2.at[:, pl.ds(WIDTH + n * HEAD_DIM, HEAD_DIM)],
            t_s.at[n], t_r.at[n], dev(h_=oh),
        )

    def start(cp):
        cp.start()
        sent.append(cp)

    def forward_head(n):
        cols = slice(n * HEAD_DIM, (n + 1) * HEAD_DIM)
        for i in range(SEQ // QCHUNK):
            rows = slice(i * QCHUNK, (i + 1) * QCHUNK)
            st = dotg(k_ref[:, cols], q_ref[rows, cols], NT) * SCALE
            e = jnp.exp(st - jnp.max(st, axis=0, keepdims=True))
            p = e * (1.0 / jnp.sum(e, axis=0, keepdims=True))
            probs[n, :, rows] = p
            t2[rows, cols] = dotg(p.astype(BF), v_ref[:, cols], TN).astype(BF)
        start(tcopy(n))

    def backward_head(n):
        cols = slice(n * HEAD_DIM, (n + 1) * HEAD_DIM)
        dk = jnp.zeros((SEQ, HEAD_DIM), F32)
        dv = jnp.zeros((SEQ, HEAD_DIM), F32)
        for i in range(SEQ // QCHUNK):
            rows = slice(i * QCHUNK, (i + 1) * QCHUNK)
            p = probs[n, :, rows]
            gh = gbuf[rows, cols]
            gp = dotg(v_ref[:, cols], gh, NT)
            rd = jnp.sum(p * gp, axis=0, keepdims=True)
            ds = (p * (gp - rd) * SCALE).astype(BF)
            dq_ref[rows, cols] = dotg(ds, k_ref[:, cols], TN).astype(BF)
            dk = dk + dot(ds, q_ref[rows, cols])
            dv = dv + dot(p.astype(BF), gh)
        dk_ref[:, cols] = dk.astype(BF)
        dv_ref[:, cols] = dv.astype(BF)

    def dcore(zp):
        s = lax.div(zp, 2)
        return rcopy(dall.at[zp], dr.at[s], dc_s.at[s], dc_r.at[s], dev(c_=oc))

    def dxcopy(zp, yh):
        s = lax.div(zp, 2)
        xj = 2 * yh + lax.div(zp, 4)
        row = lax.rem(s, 2)
        dx = lax.rem(x - xj + 4, 4)
        slot = lax.max(dx - 1, 0)
        return xj, rcopy(
            dall.at[zp, yh], xr.at[row, slot], dx_s.at[s, yh], dx_r.at[row, slot], dev(x_=xj)
        )

    def dproduct(d):
        zp = zoff(d)
        a = ag[zp].reshape(WIDTH, SEQ)
        for i in range(3):
            cols = slice(i * 256, (i + 1) * 256)
            dall[zp, :, :, cols] = dot(a, t2[:, cols]).astype(BF).reshape(2, HALF, 256)

        @pl.when(lax.rem(zp, 2) != c)
        def _():
            dcore(zp).start()

    def dpass(d):
        zp = zoff(d)

        @pl.when(lax.rem(zp, 2) == c)
        def _():
            s = lax.div(zp, 2)
            dcore(zp).wait_recv()
            for yh in range(2):
                dall[zp, yh] = (dall[zp, yh].astype(F32) + dr[s, yh].astype(F32)).astype(BF)
                xj, cp = dxcopy(zp, yh)

                @pl.when(xj != x)
                def _():
                    cp.start()

    def cproduct(d):
        zp = zoff(d)
        a = ag[zp].reshape(WIDTH, SEQ).T
        for i in range(3):
            cols = slice(i * 256, (i + 1) * 256)
            cacc[:, cols] += dot(a, wg[zp, :, :, cols].reshape(WIDTH, 256))

    at[...] = g_ref[...].T.reshape(2, HALF, SEQ)
    acopy = rcopy(at.at[oh], ag.at[z, h], a_s.at[0], a_r.at[0], dev(h_=oh))
    start(acopy)
    ag[z, h] = at[h]
    for way in range(2):
        start(zcopy(way, 0, True))
    zj = lax.rem(x, 2) * 4 + yl * 2 + c
    yj = lax.div(x, 2)
    wpcopy = rcopy(
        w_ref.at[oh], wg.at[zj, yj, :, pl.ds(WIDTH, WIDTH)], wp_s.at[0], wp_r.at[0], dev(h_=oh)
    )
    start(wpcopy)
    wg[zj, yj, :, 0:WIDTH] = w_ref[h]

    forward_head(0)

    acopy.wait_recv()
    for way in range(2):
        start(zcopy(way, 0, False))
    wpcopy.wait_recv()
    start(wycopy())
    for way in range(2):
        start(wxcopy(way, 0))
    start(wccopy(0, True))

    forward_head(1)

    def zround(k, own):
        for way in range(2):
            zcopy(way, k, own).wait_recv()
            if k < 2 or (way == 0) == own:
                start(zcopy(way, k + 1, own))

    zround(0, True)
    forward_head(2)
    wycopy().wait_recv()
    for way in range(2):
        start(wxcopy(way, 1))
    start(wccopy(0, False))
    zround(0, False)
    for way, d in ((0, 3), (1, 1)):
        wxcopy(way, 0).wait_recv()
        if way == 0:
            start(wxcopy(way, 2))
        start(wccopy(d, True))
    zround(1, True)
    for n in range(HEADS):
        tcopy(n).wait_recv()
    dproduct(0)
    zround(1, False)
    dproduct(1)
    dproduct(-1)
    for way, d in ((0, 3), (1, 1)):
        wxcopy(way, 1).wait_recv()
        if way == 1:
            start(wxcopy(way, 2))
        start(wccopy(d, False))
    dpass(0)
    zround(2, True)
    dpass(1)
    dpass(-1)
    dproduct(2)
    dproduct(-2)
    zround(2, False)
    dpass(2)
    dpass(-2)
    dproduct(3)
    dproduct(-3)
    wxcopy(0, 2).wait_recv()
    start(wccopy(2, True))
    wxcopy(1, 2).wait_recv()
    start(wccopy(2, False))
    dpass(3)
    dpass(-3)
    for d in range(4):
        for own_row in (True, False):
            wccopy(d, own_row).wait_recv()
    cacc[...] = jnp.zeros_like(cacc)

    @pl.loop(-3, 4)
    def _(d):
        cproduct(d)

    zcopy(0, 3, True).wait_recv()
    zcopy(1, 3, False).wait_recv()
    cproduct(4)
    csend[...] = cacc[:, WIDTH : 2 * WIDTH].astype(BF)
    ccopy = rcopy(csend, crecv, c_s.at[0], c_r.at[0], dev(h_=oh))
    start(ccopy)
    dproduct(4)
    dpass(4)
    ccopy.wait_recv()
    gbuf[...] = (cacc[:, 0:WIDTH] + crecv[...].astype(F32)).astype(BF)
    backward_head(0)

    def total(row):
        zf = lax.rem(x, 2) * 4 + row * 2 + c
        yh = lax.div(x, 2)
        for i in range(3):
            rcopy(xr.at[row, i], xr.at[row, i], dx_s.at[0, 0], dx_r.at[row, i], dev(x_=xoff(1))).wait_recv()
        acc = dall[zf, yh].astype(F32)
        for i in range(3):
            acc = acc + xr[row, i].astype(F32)
        return acc

    def ycopy(i):
        to = (dev(yl_=oyl), dev(yl_=oyl, h_=oh), dev(h_=oh))[i]
        return rcopy(fs.at[i], yr.at[i], dy_s.at[i], dy_r.at[i], to)

    other = total(oyl)
    fs[0] = other[:, 0:WIDTH].astype(BF)
    fs[1] = other[:, WIDTH:].astype(BF)
    start(ycopy(0))
    start(ycopy(1))
    mine = total(yl)
    fs[2] = mine[:, WIDTH:].astype(BF)
    start(ycopy(2))
    fkeep[...] = mine[:, 0:WIDTH]
    backward_head(1)
    backward_head(2)
    for i in range(3):
        ycopy(i).wait_recv()
    dw_ref[h] = fkeep[...] + yr[0].astype(F32)
    dw_ref[oh] = yr[1].astype(F32) + yr[2].astype(F32)

    for cp in sent:
        cp.wait_send()
    for s in range(4):
        dcore(2 * s + oc).wait_send()
        for yh in range(2):
            xj, cp = dxcopy(2 * s + c, yh)

            @pl.when(xj != x)
            def _():
                cp.wait_send()


def shards(queries, keys, values, grad_out, out_weight):
    vmem = pl.BlockSpec(memory_space=pltpu.VMEM)
    dma = pltpu.SemaphoreType.DMA
    pairs = [
        (2, 8), (1,), (1,), (1,), (2, 3), (8,),
        (3,), (1,),
    ]
    sems = []
    for shape in pairs:
        sems += [dma(shape), dma(shape)]
    sems += [dma((4,)), dma((4,)), dma((4, 2)), dma((2, 3)), dma((3,)), dma((3,))]
    d_queries, d_keys, d_values, d_weight = pl.pallas_call(
        kernel,
        out_shape=(
            jax.ShapeDtypeStruct((SEQ, WIDTH), BF),
            jax.ShapeDtypeStruct((SEQ, WIDTH), BF),
            jax.ShapeDtypeStruct((SEQ, WIDTH), BF),
            jax.ShapeDtypeStruct((2, HALF, WIDTH), F32),
        ),
        in_specs=[vmem] * 5,
        out_specs=(vmem,) * 4,
        scratch_shapes=[
            pltpu.VMEM((2, HALF, SEQ), BF),
            pltpu.VMEM((8, 2, HALF, SEQ), BF),
            pltpu.VMEM((8, 2, HALF, 2 * WIDTH), BF),
            pltpu.VMEM((SEQ, 2 * WIDTH), BF),
            pltpu.VMEM((HEADS, SEQ, SEQ), F32),
            pltpu.VMEM((SEQ, 2 * WIDTH), F32),
            pltpu.VMEM((SEQ, WIDTH), BF),
            pltpu.VMEM((SEQ, WIDTH), BF),
            pltpu.VMEM((SEQ, WIDTH), BF),
            pltpu.VMEM((8, 2, HALF, 2 * WIDTH), BF),
            pltpu.VMEM((4, 2, HALF, 2 * WIDTH), BF),
            pltpu.VMEM((2, 3, HALF, 2 * WIDTH), BF),
            pltpu.VMEM((3, HALF, WIDTH), BF),
            pltpu.VMEM((3, HALF, WIDTH), BF),
            pltpu.VMEM((HALF, WIDTH), F32),
        ]
        + sems,
        compiler_params=pltpu.CompilerParams(
            collective_id=1, has_side_effects=True, vmem_limit_bytes=48 << 20
        ),
        cost_estimate=pl.CostEstimate(
            flops=6_000_000_000, bytes_accessed=4_000_000, transcendentals=800_000
        ),
    )(queries, keys, values, grad_out, out_weight.reshape(2, HALF, WIDTH))
    return d_queries, d_keys, d_values, d_weight.reshape(WIDTH, WIDTH)


def solution(mesh):
    placed = P("fsdp", "tensor")
    return jax.shard_map(
        shards,
        mesh=mesh,
        in_specs=(placed,) * 5,
        out_specs=(placed,) * 4,
        check_vma=False,
    )
```

```python
import functools

import jax
import jax.numpy as jnp
from jax import lax
from jax.experimental import pallas as pl
from jax.experimental.pallas import tpu as pltpu
from jax.sharding import PartitionSpec as P

HEAD_DIM = 128
SCALE = HEAD_DIM ** (-0.5)
MESH = pl.DeviceIdType.MESH
BF = jnp.bfloat16
F32 = jnp.float32
TN = (((0,), (0,)), ((), ()))
NT = (((1,), (1,)), ((), ()))

SEQ = 512
WIDTH = 384
HALF = 192
HEADS = 3
QCHUNK = 256


def dot(a, b):
    return jnp.dot(a, b, preferred_element_type=F32)


def dotg(a, b, dims):
    return lax.dot_general(a, b, dims, preferred_element_type=F32)


def kernel(
    q_hbm, k_hbm, v_hbm, g_hbm, w_hbm,
    dq_ref, dk_ref, dv_ref, dw_ref,
    q_ref, k_ref, v_ref, g_ref, w_ref,
    at, ag, an, wg, t2, probs, cacc, csend, crecv, gbuf, dall, dr, xr, fs, yr, fkeep,
    in_s,
    z_s, z_r, a_s, a_r, wp_s, wp_r, wy_s, wy_r, wx_s, wx_r, wc_s, wc_r,
    t_s, t_r, c_s, c_r, dc_s, dc_r, dx_s, dx_r, dy_s, dy_r,
):
    f = lax.axis_index("fsdp")
    t = lax.axis_index("tensor")
    x = lax.div(f, 4)
    yl = lax.rem(lax.div(f, 2), 2)
    c = lax.rem(f, 2)
    h = lax.div(t, 8)
    z = lax.rem(t, 8)
    oh = 1 - h
    oyl = 1 - yl
    oc = 1 - c

    def dev(x_=None, yl_=None, c_=None, h_=None, z_=None):
        x_ = x if x_ is None else x_
        yl_ = yl if yl_ is None else yl_
        c_ = c if c_ is None else c_
        h_ = h if h_ is None else h_
        z_ = z if z_ is None else z_
        return (x_ * 4 + yl_ * 2 + c_, h_ * 8 + z_)

    def zoff(d):
        return lax.rem(z + 8 + d, 8)

    def xoff(d):
        return lax.rem(x + 4 + d, 4)

    def rcopy(src, dst, ssem, rsem, device):
        return pltpu.make_async_remote_copy(
            src_ref=src, dst_ref=dst, send_sem=ssem, recv_sem=rsem,
            device_id=device, device_id_type=MESH,
        )

    loads = {}
    for i, (name, src, dst) in enumerate((
        ("g", g_hbm, g_ref), ("w", w_hbm, w_ref), ("k", k_hbm, k_ref),
        ("q", q_hbm, q_ref), ("v", v_hbm, v_ref),
    )):
        loads[name] = pltpu.make_async_copy(src, dst, in_s.at[i])
        loads[name].start()

    peers = [
        dev(z_=zoff(1)), dev(z_=zoff(-1)),
        dev(h_=oh), dev(yl_=oyl), dev(yl_=oyl, h_=oh),
        dev(x_=xoff(1)), dev(x_=xoff(-1)), dev(x_=xoff(2)),
        dev(c_=oc),
    ]
    barrier = pltpu.get_barrier_semaphore()
    for peer in peers:
        pl.semaphore_signal(barrier, inc=1, device_id=peer, device_id_type=MESH)

    sent = []

    def start(cp):
        cp.start()
        sent.append(cp)

    def zcopy(way, k, own):
        src = zoff(-k) if way == 0 else zoff(k)
        piece = h if own else oh
        to = dev(z_=zoff(1)) if way == 0 else dev(z_=zoff(-1))
        i = 2 * k + (0 if own else 1)
        ref = ag.at[src, piece]
        return rcopy(ref, ref, z_s.at[way, i], z_r.at[way, i], to)

    def wblock(x_, yl_, part):
        return wg.at[lax.rem(x_, 2) * 4 + yl_ * 2 + c, part, lax.div(x_, 2)]

    def wycopy(d, part):
        ref = wblock(xoff(d), yl, part)
        return rcopy(ref, ref, wy_s.at[d, part], wy_r.at[d, part], dev(yl_=oyl))

    def wxcopy(way, i, part):
        to = dev(x_=xoff(1)) if way == 0 else dev(x_=xoff(-1))
        if i == 0:
            ref = wblock(x, yl, part)
        elif i == 1:
            ref = wblock(x, oyl, part)
        elif part == 0:
            ref = wblock(xoff(-1), yl, part) if way == 0 else wblock(xoff(1), oyl, part)
        else:
            ref = wblock(xoff(-1 if way == 0 else 1), yl, part)
            ref = ref.at[pl.ds(way * (HALF // 2), HALF // 2)]
        return rcopy(ref, ref, wx_s.at[way, i, part], wx_r.at[way, i, part], to)

    def wccopy(d, own_row, part):
        ref = wblock(xoff(d), yl if own_row else oyl, part)
        i = 2 * d + (0 if own_row else 1)
        return rcopy(ref, ref, wc_s.at[i, part], wc_r.at[i, part], dev(c_=oc))

    def tcopy(n):
        return rcopy(t2.at[n], t2.at[HEADS + n], t_s.at[n], t_r.at[n], dev(h_=oh))

    def ccopy(n):
        return rcopy(csend.at[n], crecv.at[n], c_s.at[n], c_r.at[n], dev(h_=oh))

    def forward_head(n):
        cols = slice(n * HEAD_DIM, (n + 1) * HEAD_DIM)
        for i in range(SEQ // QCHUNK):
            rows = slice(i * QCHUNK, (i + 1) * QCHUNK)
            st = dotg(k_ref[:, cols], q_ref[rows, cols], NT) * SCALE
            e = jnp.exp(st - jnp.max(st, axis=0, keepdims=True))
            p = e * (1.0 / jnp.sum(e, axis=0, keepdims=True))
            probs[n, :, rows] = p
            t2[n, rows] = dotg(p.astype(BF), v_ref[:, cols], TN).astype(BF)
        start(tcopy(n))

    def backward_head(n):
        cols = slice(n * HEAD_DIM, (n + 1) * HEAD_DIM)
        ccopy(n).wait_recv()
        gbuf[:, cols] = (cacc[0, :, cols] + crecv[n].astype(F32)).astype(BF)
        dk = jnp.zeros((SEQ, HEAD_DIM), F32)
        dv = jnp.zeros((SEQ, HEAD_DIM), F32)
        for i in range(SEQ // QCHUNK):
            rows = slice(i * QCHUNK, (i + 1) * QCHUNK)
            p = probs[n, :, rows]
            gh = gbuf[rows, cols]
            gp = dotg(v_ref[:, cols], gh, NT)
            rd = jnp.sum(p * gp, axis=0, keepdims=True)
            ds = (p * (gp - rd) * SCALE).astype(BF)
            dq_ref[rows, cols] = dotg(ds, k_ref[:, cols], TN).astype(BF)
            dk = dk + dot(ds, q_ref[rows, cols])
            dv = dv + dot(p.astype(BF), gh)
        dk_ref[:, cols] = dk.astype(BF)
        dv_ref[:, cols] = dv.astype(BF)

    def dcore(zp, part):
        s = lax.div(zp, 2)
        return rcopy(
            dall.at[zp, part], dr.at[s, part], dc_s.at[s, part], dc_r.at[s, part], dev(c_=oc)
        )

    def dxcopy(zp, part, yh):
        s = lax.div(zp, 2)
        xj = 2 * yh + lax.div(zp, 4)
        row = lax.rem(s, 2)
        slot = lax.max(lax.rem(x - xj + 4, 4) - 1, 0)
        return xj, rcopy(
            dall.at[zp, part, yh], xr.at[row, slot, part],
            dx_s.at[s, part, yh], dx_r.at[row, slot, part], dev(x_=xj),
        )

    def dproduct(part, *ds):
        b = jnp.concatenate([t2[part * HEADS + n] for n in range(HEADS)], axis=1)
        for d in ds:
            zp = zoff(d)
            for yh in range(2):
                dall[zp, part, yh] = dot(ag[zp, yh], b).astype(BF)

            @pl.when(lax.rem(zp, 2) != c)
            def _():
                dcore(zp, part).start()

    def dpass(part, *ds):
        for d in ds:
            zp = zoff(d)

            @pl.when(lax.rem(zp, 2) == c)
            def _():
                s = lax.div(zp, 2)
                dcore(zp, part).wait_recv()
                for yh in range(2):
                    dall[zp, part, yh] = (
                        dall[zp, part, yh].astype(F32) + dr[s, part, yh].astype(F32)
                    ).astype(BF)
                    xj, cp = dxcopy(zp, part, yh)

                    @pl.when(xj != x)
                    def _():
                        cp.start()

    def total(row, part):
        zf = lax.rem(x, 2) * 4 + row * 2 + c
        yh = lax.div(x, 2)
        acc = dall[zf, part, yh].astype(F32)
        for i in range(3):
            rcopy(
                xr.at[row, i, part], xr.at[row, i, part], dx_s.at[0, 0, 0],
                dx_r.at[row, i, part], dev(x_=xoff(1)),
            ).wait_recv()
            acc = acc + xr[row, i, part].astype(F32)
        return acc

    def ycopy(i):
        to = (dev(yl_=oyl), dev(yl_=oyl, h_=oh), dev(h_=oh))[i]
        return rcopy(fs.at[i], yr.at[i], dy_s.at[i], dy_r.at[i], to)

    def transposed(d):
        zp = zoff(d)
        an[zp] = ag[zp].reshape(WIDTH, SEQ).T

    def cproduct(part, ds):
        for i in range(2):
            rows = slice(i * 256, (i + 1) * 256)
            acc = cacc[part, rows]
            for d in ds:
                zp = zoff(d)
                acc = acc + dot(an[zp, rows], wg[zp, part].reshape(WIDTH, WIDTH))
            cacc[part, rows] = acc

    def zround(k, own):
        for way in range(2):
            zcopy(way, k, own).wait_recv()
            if k < 2 or (way == 0) == own:
                start(zcopy(way, k + 1, own))

    def wrow():
        wycopy(0, 0).wait_recv()
        for way in range(2):
            start(wxcopy(way, 1, 0))
        start(wccopy(0, False, 0))

    def wnear(i):
        for way, d in ((0, 3), (1, 1)):
            wxcopy(way, i, 0).wait_recv()
            if way == i:
                start(wxcopy(way, 2, 0))
            start(wccopy(d, i == 0, 0))

    def wfar():
        for way in range(2):
            wxcopy(way, 2, 0).wait_recv()
            start(wccopy(2, way == 0, 0))

    def wpartner():
        wpcopy.wait_recv()
        for way in range(2):
            start(wxcopy(way, 0, 1))
        start(wycopy(0, 1))
        start(wccopy(0, True, 1))

    def pnear():
        for way, d in ((0, 3), (1, 1)):
            wxcopy(way, 0, 1).wait_recv()
            start(wxcopy(way, 2, 1))
            start(wycopy(d, 1))
            start(wccopy(d, True, 1))

    def pfar():
        for way in range(2):
            wxcopy(way, 2, 1).wait_recv()
        start(wycopy(2, 1))
        start(wccopy(2, True, 1))

    def prow():
        for d in (0, 3, 1, 2):
            wycopy(d, 1).wait_recv()
            start(wccopy(d, False, 1))

    def tready():
        for n in range(HEADS):
            tcopy(n).wait_recv()

    def wdone(part):
        for d in range(4):
            for own_row in (True, False):
                wccopy(d, own_row, part).wait_recv()

    def zlast():
        zcopy(0, 3, True).wait_recv()
        zcopy(1, 3, False).wait_recv()

    zj = lax.rem(x, 2) * 4 + yl * 2 + c
    yj = lax.div(x, 2)
    loads["g"].wait()
    at[...] = g_ref[...].T.reshape(2, HALF, SEQ)
    ag[z, h] = at[h]
    loads["w"].wait()
    wg[zj, 0, yj] = w_ref[h]
    pl.semaphore_wait(barrier, len(peers))

    acopy = rcopy(at.at[oh], ag.at[z, h], a_s.at[0], a_r.at[0], dev(h_=oh))
    start(acopy)
    start(wycopy(0, 0))
    for way in range(2):
        start(zcopy(way, 0, True))
        start(wxcopy(way, 0, 0))
    wpcopy = rcopy(w_ref.at[oh], wg.at[zj, 1, yj], wp_s.at[0], wp_r.at[0], dev(h_=oh))
    start(wpcopy)
    start(wccopy(0, True, 0))

    for name in ("k", "q", "v"):
        loads[name].wait()
    forward_head(0)
    forward_head(1)
    forward_head(2)
    cacc[...] = jnp.zeros_like(cacc)
    zround(0, True)
    wrow()
    wnear(0)
    acopy.wait_recv()
    for way in range(2):
        start(zcopy(way, 0, False))
    dproduct(0, 0)
    wnear(1)
    zround(1, True)
    wpartner()
    dpass(0, 0)
    zround(0, False)
    dproduct(0, 1, -1)
    wfar()
    transposed(0)
    zround(2, True)
    dpass(0, 1, -1)
    pnear()
    zround(1, False)
    dproduct(0, 2, -2)
    transposed(1)
    transposed(-1)
    tready()
    dproduct(1, 0, 1, -1)
    dpass(0, 2, -2)
    pfar()
    dpass(1, 0)
    dproduct(1, 2, -2)
    dpass(1, 1, -1)
    zround(2, False)
    dproduct(0, 3, -3)
    dpass(1, 2, -2)
    dproduct(1, 3, -3)
    transposed(2)
    transposed(-2)
    dpass(0, 3, -3)
    wdone(0)
    cproduct(0, range(-2, 3))
    transposed(3)
    transposed(-3)
    dpass(1, 3, -3)
    prow()
    wdone(1)
    cproduct(1, range(-3, 4))
    zlast()
    transposed(4)
    cproduct(1, [4])
    for n in range(HEADS):
        csend[n] = cacc[1, :, pl.ds(n * HEAD_DIM, HEAD_DIM)].astype(BF)
        start(ccopy(n))
    dproduct(0, 4)
    dproduct(1, 4)
    cproduct(0, [-3, 3, 4])
    dpass(0, 4)
    dpass(1, 4)
    backward_head(0)
    fs[0] = total(oyl, 0).astype(BF)
    start(ycopy(0))
    fs[1] = total(oyl, 1).astype(BF)
    start(ycopy(1))
    fs[2] = total(yl, 1).astype(BF)
    start(ycopy(2))
    backward_head(1)
    fkeep[...] = total(yl, 0)
    backward_head(2)
    for i in range(3):
        ycopy(i).wait_recv()
    dw_ref[h] = fkeep[...] + yr[0].astype(F32)
    dw_ref[oh] = yr[1].astype(F32) + yr[2].astype(F32)

    for cp in sent:
        cp.wait_send()
    for s in range(4):
        for part in range(2):
            dcore(2 * s + oc, part).wait_send()
            for yh in range(2):
                xj, cp = dxcopy(2 * s + c, part, yh)

                @pl.when(xj != x)
                def _():
                    cp.wait_send()


def shards(queries, keys, values, grad_out, out_weight):
    vmem = pl.BlockSpec(memory_space=pltpu.VMEM)
    hbm = pl.BlockSpec(memory_space=pltpu.HBM)
    dma = pltpu.SemaphoreType.DMA
    pairs = [
        (2, 8), (1,), (1,), (4, 2), (2, 3, 2), (8, 2),
        (3,), (3,), (4, 2),
    ]
    sems = [dma((5,))]
    for shape in pairs:
        sems += [dma(shape), dma(shape)]
    sems += [dma((4, 2, 2)), dma((2, 3, 2)), dma((3,)), dma((3,))]
    block = pltpu.VMEM((SEQ, WIDTH), BF)
    operands = (queries, keys, values, grad_out, out_weight.reshape(2, HALF, WIDTH))
    operands = [pltpu.with_memory_space_constraint(a, pltpu.HBM) for a in operands]
    d_queries, d_keys, d_values, d_weight = pl.pallas_call(
        kernel,
        out_shape=(
            jax.ShapeDtypeStruct((SEQ, WIDTH), BF),
            jax.ShapeDtypeStruct((SEQ, WIDTH), BF),
            jax.ShapeDtypeStruct((SEQ, WIDTH), BF),
            jax.ShapeDtypeStruct((2, HALF, WIDTH), F32),
        ),
        in_specs=[hbm] * 5,
        out_specs=(vmem,) * 4,
        scratch_shapes=[
            block,
            block,
            block,
            block,
            pltpu.VMEM((2, HALF, WIDTH), BF),
            pltpu.VMEM((2, HALF, SEQ), BF),
            pltpu.VMEM((8, 2, HALF, SEQ), BF),
            pltpu.VMEM((8, SEQ, WIDTH), BF),
            pltpu.VMEM((8, 2, 2, HALF, WIDTH), BF),
            pltpu.VMEM((2 * HEADS, SEQ, HEAD_DIM), BF),
            pltpu.VMEM((HEADS, SEQ, SEQ), F32),
            pltpu.VMEM((2, SEQ, WIDTH), F32),
            pltpu.VMEM((HEADS, SEQ, HEAD_DIM), BF),
            pltpu.VMEM((HEADS, SEQ, HEAD_DIM), BF),
            block,
            pltpu.VMEM((8, 2, 2, HALF, WIDTH), BF),
            pltpu.VMEM((4, 2, 2, HALF, WIDTH), BF),
            pltpu.VMEM((2, 3, 2, HALF, WIDTH), BF),
            pltpu.VMEM((3, HALF, WIDTH), BF),
            pltpu.VMEM((3, HALF, WIDTH), BF),
            pltpu.VMEM((HALF, WIDTH), F32),
        ]
        + sems,
        compiler_params=pltpu.CompilerParams(
            collective_id=1, has_side_effects=True, vmem_limit_bytes=44 << 20
        ),
        cost_estimate=pl.CostEstimate(
            flops=6_000_000_000, bytes_accessed=4_000_000, transcendentals=800_000
        ),
    )(*operands)
    return d_queries, d_keys, d_values, d_weight.reshape(WIDTH, WIDTH)


def solution(mesh):
    placed = P("fsdp", "tensor")
    return jax.shard_map(
        shards,
        mesh=mesh,
        in_specs=(placed,) * 5,
        out_specs=(placed,) * 4,
        check_vma=False,
    )
```

```python
import functools

import jax
import jax.numpy as jnp
from jax import lax
from jax.experimental import pallas as pl
from jax.experimental.pallas import tpu as pltpu
from jax.sharding import PartitionSpec as P

HEAD_DIM = 128
SCALE = HEAD_DIM ** (-0.5)
MESH = pl.DeviceIdType.MESH
BF = jnp.bfloat16
F32 = jnp.float32
TN = (((0,), (0,)), ((), ()))
NT = (((1,), (1,)), ((), ()))

SEQ = 512
WIDTH = 384
HALF = 192
RELAYED = (0, 1, -1, 2, -2)
HEADS = 3
QCHUNK = 256


def dot(a, b):
    return jnp.dot(a, b, preferred_element_type=F32)


def dotg(a, b, dims):
    return lax.dot_general(a, b, dims, preferred_element_type=F32)


def kernel(
    q_hbm, k_hbm, v_hbm, g_hbm, w_hbm,
    dq_ref, dk_ref, dv_ref, dw_ref,
    q_ref, k_ref, v_ref, g_ref, w_ref,
    at, ag, an, wg, t2, probs, cacc, csend, crecv, gbuf, dall, dr, xp, xr, fs, yr, fkeep,
    in_s,
    z_s, z_r, a_s, a_r, wp_s, wp_r, wy_s, wy_r, wx_s, wx_r, wc_s, wc_r,
    t_s, t_r, c_s, c_r, dc_s, dc_r, dp_s, dp_r, dx_s, dx_r, dy_s, dy_r,
):
    f = lax.axis_index("fsdp")
    t = lax.axis_index("tensor")
    x = lax.div(f, 4)
    yl = lax.rem(lax.div(f, 2), 2)
    c = lax.rem(f, 2)
    h = lax.div(t, 8)
    z = lax.rem(t, 8)
    oh = 1 - h
    oyl = 1 - yl
    oc = 1 - c

    def dev(x_=None, yl_=None, c_=None, h_=None, z_=None):
        x_ = x if x_ is None else x_
        yl_ = yl if yl_ is None else yl_
        c_ = c if c_ is None else c_
        h_ = h if h_ is None else h_
        z_ = z if z_ is None else z_
        return (x_ * 4 + yl_ * 2 + c_, h_ * 8 + z_)

    def zoff(d):
        return lax.rem(z + 8 + d, 8)

    def xoff(d):
        return lax.rem(x + 4 + d, 4)

    def rcopy(src, dst, ssem, rsem, device):
        return pltpu.make_async_remote_copy(
            src_ref=src, dst_ref=dst, send_sem=ssem, recv_sem=rsem,
            device_id=device, device_id_type=MESH,
        )

    loads = {}
    for i, (name, src, dst) in enumerate((
        ("g", g_hbm, g_ref), ("w", w_hbm, w_ref), ("k", k_hbm, k_ref),
        ("q", q_hbm, q_ref), ("v", v_hbm, v_ref),
    )):
        loads[name] = pltpu.make_async_copy(src, dst, in_s.at[i])
        loads[name].start()

    peers = [
        dev(z_=zoff(1)), dev(z_=zoff(-1)),
        dev(h_=oh), dev(yl_=oyl), dev(yl_=oyl, h_=oh),
        dev(x_=xoff(1)), dev(x_=xoff(-1)), dev(x_=xoff(2)),
        dev(c_=oc),
    ]
    barrier = pltpu.get_barrier_semaphore()
    for peer in peers:
        pl.semaphore_signal(barrier, inc=1, device_id=peer, device_id_type=MESH)

    sent = []

    def start(cp):
        cp.start()
        sent.append(cp)

    def zcopy(way, k, half):
        src = zoff(-k) if way == 0 else zoff(k)
        to = dev(z_=zoff(1)) if way == 0 else dev(z_=zoff(-1))
        if half is None:
            i = 8 + k
            ref = ag.at[src, oh]
        else:
            i = 2 * k + half
            ref = ag.at[src, h, pl.ds(half * (HALF // 2), HALF // 2)]
        return rcopy(ref, ref, z_s.at[way, i], z_r.at[way, i], to)

    def wblock(x_, yl_, part):
        return wg.at[lax.rem(x_, 2) * 4 + yl_ * 2 + c, part, lax.div(x_, 2)]

    def wycopy(d, part):
        ref = wblock(xoff(d), yl, part)
        return rcopy(ref, ref, wy_s.at[d, part], wy_r.at[d, part], dev(yl_=oyl))

    def wpcopy(same_row):
        i = 0 if same_row else 1
        to = dev(h_=oh) if same_row else dev(yl_=oyl, h_=oh)
        return rcopy(w_ref.at[oh], wblock(x, yl, 1), wp_s.at[i], wp_r.at[i], to)

    def wxcopy(way, i, part):
        to = dev(x_=xoff(1)) if way == 0 else dev(x_=xoff(-1))
        if i == 0:
            ref = wblock(x, yl, part)
        elif i == 1:
            ref = wblock(x, oyl, part)
        elif part == 0:
            ref = wblock(xoff(-1), yl, part) if way == 0 else wblock(xoff(1), oyl, part)
        else:
            ref = wblock(xoff(-1 if way == 0 else 1), yl, part)
            ref = ref.at[pl.ds(way * (HALF // 2), HALF // 2)]
        return rcopy(ref, ref, wx_s.at[way, i, part], wx_r.at[way, i, part], to)

    def wccopy(d, own_row, part):
        ref = wblock(xoff(d), yl if own_row else oyl, part)
        i = 2 * d + (0 if own_row else 1)
        return rcopy(ref, ref, wc_s.at[i, part], wc_r.at[i, part], dev(c_=oc))

    def tcopy(n):
        return rcopy(t2.at[n], t2.at[HEADS + n], t_s.at[n], t_r.at[n], dev(h_=oh))

    def ccopy(n):
        return rcopy(csend.at[n], crecv.at[n], c_s.at[n], c_r.at[n], dev(h_=oh))

    def forward_head(n):
        cols = slice(n * HEAD_DIM, (n + 1) * HEAD_DIM)
        for i in range(SEQ // QCHUNK):
            rows = slice(i * QCHUNK, (i + 1) * QCHUNK)
            st = dotg(k_ref[:, cols], q_ref[rows, cols], NT) * SCALE
            e = jnp.exp(st - jnp.max(st, axis=0, keepdims=True))
            p = e * (1.0 / jnp.sum(e, axis=0, keepdims=True))
            probs[n, :, rows] = p
            t2[n, rows] = dotg(p.astype(BF), v_ref[:, cols], TN).astype(BF)
        start(tcopy(n))

    def backward_head(n):
        cols = slice(n * HEAD_DIM, (n + 1) * HEAD_DIM)
        ccopy(n).wait_recv()
        gbuf[:, cols] = (cacc[0, :, cols] + crecv[n].astype(F32)).astype(BF)
        dk = jnp.zeros((SEQ, HEAD_DIM), F32)
        dv = jnp.zeros((SEQ, HEAD_DIM), F32)
        for i in range(SEQ // QCHUNK):
            rows = slice(i * QCHUNK, (i + 1) * QCHUNK)
            p = probs[n, :, rows]
            gh = gbuf[rows, cols]
            gp = dotg(v_ref[:, cols], gh, NT)
            rd = jnp.sum(p * gp, axis=0, keepdims=True)
            ds = (p * (gp - rd) * SCALE).astype(BF)
            dq_ref[rows, cols] = dotg(ds, k_ref[:, cols], TN).astype(BF)
            dk = dk + dot(ds, q_ref[rows, cols])
            dv = dv + dot(p.astype(BF), gh)
        dk_ref[:, cols] = dk.astype(BF)
        dv_ref[:, cols] = dv.astype(BF)

    def dcore(zp, part):
        s = lax.div(zp, 2)
        return rcopy(
            dall.at[zp, part], dr.at[s, part], dc_s.at[s, part], dc_r.at[s, part], dev(c_=oc)
        )

    def dxcopy(zp, part, yh):
        s = lax.div(zp, 2)
        xj = 2 * yh + lax.div(zp, 4)
        row = lax.rem(s, 2)
        slot = lax.max(lax.rem(x - xj + 4, 4) - 1, 0)
        return xj, rcopy(
            dall.at[zp, part, yh], xr.at[row, slot, part],
            dx_s.at[s, part, yh], dx_r.at[row, slot, part], dev(x_=xj),
        )

    def dproduct(part, *ds):
        b = jnp.concatenate([t2[part * HEADS + n] for n in range(HEADS)], axis=1)
        for d in ds:
            zp = zoff(d)
            for yh in range(2):
                dall[zp, part, yh] = dot(ag[zp, yh], b).astype(BF)

            @pl.when(lax.rem(zp, 2) != c)
            def _():
                dcore(zp, part).start()

    def even(zp):
        return lax.rem(x, 2) == lax.div(zp, 4)

    def is_relayed(d):
        return d in RELAYED

    def dpcopy(zp, d, part, half):
        i = RELAYED.index(d)
        src = dall.at[zp, part, 1 - lax.div(x, 2), pl.ds(half * (HALF // 2), HALF // 2)]
        to = dev(x_=xoff(-1)) if half == 0 else dev(x_=xoff(1))
        return rcopy(
            src, xp.at[i, part, half], dp_s.at[i, part, half], dp_r.at[i, part, half], to
        )

    def dpass(part, *ds):
        for d in ds:
            zp = zoff(d)

            @pl.when(lax.rem(zp, 2) == c)
            def _():
                s = lax.div(zp, 2)
                dcore(zp, part).wait_recv()
                for yh in range(2):
                    dall[zp, part, yh] = (
                        dall[zp, part, yh].astype(F32) + dr[s, part, yh].astype(F32)
                    ).astype(BF)
                    if not is_relayed(d):
                        xj, cp = dxcopy(zp, part, yh)

                        @pl.when(xj != x)
                        def _():
                            cp.start()

                if is_relayed(d):

                    @pl.when(even(zp))
                    def _():
                        for half in range(2):
                            dpcopy(zp, d, part, half).start()

    def drelay(part, *ds):
        for d in ds:
            zp = zoff(d)

            @pl.when((lax.rem(zp, 2) == c) & jnp.logical_not(even(zp)))
            def _():
                for half in range(2):
                    dpcopy(zp, d, part, half).wait_recv()
                    yh = lax.div(xoff(-1) if half == 0 else xoff(1), 2)
                    rows = pl.ds(half * (HALF // 2), HALF // 2)
                    dall[zp, part, yh, rows] = (
                        dall[zp, part, yh, rows].astype(F32)
                        + xp[RELAYED.index(d), part, half].astype(F32)
                    ).astype(BF)
                    dxcopy(zp, part, yh)[1].start()

    def total(row, part):
        zf = lax.rem(x, 2) * 4 + row * 2 + c
        yh = lax.div(x, 2)
        away = lax.rem(zf - z + 8, 8)
        relayed = (away <= 2) | (away >= 6)
        for i in range(3):
            arrival = rcopy(
                xr.at[row, i, part], xr.at[row, i, part], dx_s.at[0, 0, 0],
                dx_r.at[row, i, part], dev(x_=xoff(1)),
            )
            if i == 1:

                @pl.when(jnp.logical_not(relayed))
                def _():
                    arrival.wait_recv()

                @pl.when(relayed)
                def _():
                    xr[row, 1, part] = jnp.zeros((HALF, WIDTH), BF)

            else:
                arrival.wait_recv()
        acc = dall[zf, part, yh].astype(F32)
        for i in range(3):
            acc = acc + xr[row, i, part].astype(F32)
        return acc

    def ycopy(i):
        to = (dev(yl_=oyl), dev(yl_=oyl, h_=oh), dev(h_=oh))[i]
        return rcopy(fs.at[i], yr.at[i], dy_s.at[i], dy_r.at[i], to)

    def transposed(d):
        zp = zoff(d)
        an[zp] = ag[zp].reshape(WIDTH, SEQ).T

    def cproduct(part, ds):
        for i in range(2):
            rows = slice(i * 256, (i + 1) * 256)
            acc = cacc[part, rows]
            for d in ds:
                zp = zoff(d)
                acc = acc + dot(an[zp, rows], wg[zp, part].reshape(WIDTH, WIDTH))
            cacc[part, rows] = acc

    def zround(k, own):
        for half in (0, 1) if own else (None,):
            for way in range(2):
                zcopy(way, k, half).wait_recv()
                if k < 2 or (way == 0) == own:
                    start(zcopy(way, k + 1, half))

    def wsend(own_row, part):
        for way in range(2):
            start(wxcopy(way, 0 if own_row else 1, part))
        start(wccopy(0, own_row, part))

    def wrow():
        wycopy(0, 0).wait_recv()
        wsend(False, 0)

    def wpartner(same_row):
        wpcopy(same_row).wait_recv()
        if same_row:
            wsend(True, 1)
        else:
            start(wccopy(0, False, 1))

    def wnear(i):
        for way, d in ((0, 3), (1, 1)):
            wxcopy(way, i, 0).wait_recv()
            if way == i:
                start(wxcopy(way, 2, 0))
            start(wccopy(d, i == 0, 0))

    def wfar():
        for way in range(2):
            wxcopy(way, 2, 0).wait_recv()
            start(wccopy(2, way == 0, 0))

    def pnear():
        for way, d in ((0, 3), (1, 1)):
            wxcopy(way, 0, 1).wait_recv()
            start(wxcopy(way, 2, 1))
            start(wycopy(d, 1))
            start(wccopy(d, True, 1))

    def pfar():
        for way in range(2):
            wxcopy(way, 2, 1).wait_recv()
        start(wycopy(2, 1))
        start(wccopy(2, True, 1))

    def prow():
        for d in (3, 1, 2):
            wycopy(d, 1).wait_recv()
            start(wccopy(d, False, 1))

    def tready():
        for n in range(HEADS):
            tcopy(n).wait_recv()

    def wdone(part):
        for d in range(4):
            for own_row in (True, False):
                wccopy(d, own_row, part).wait_recv()

    def zlast():
        zcopy(0, 3, 0).wait_recv()
        zcopy(0, 3, 1).wait_recv()
        zcopy(1, 3, None).wait_recv()

    zj = lax.rem(x, 2) * 4 + yl * 2 + c
    yj = lax.div(x, 2)
    loads["g"].wait()
    at[...] = g_ref[...].T.reshape(2, HALF, SEQ)
    ag[z, h] = at[h]
    loads["w"].wait()
    wg[zj, 0, yj] = w_ref[h]
    pl.semaphore_wait(barrier, len(peers))

    acopy = rcopy(at.at[oh], ag.at[z, h], a_s.at[0], a_r.at[0], dev(h_=oh))
    start(acopy)
    for half in range(2):
        for way in range(2):
            start(zcopy(way, 0, half))
    for way in range(2):
        start(wxcopy(way, 0, 0))
    start(wycopy(0, 0))
    start(wpcopy(False))
    start(wpcopy(True))
    start(wccopy(0, True, 0))

    for name in ("k", "q", "v"):
        loads[name].wait()
    forward_head(0)
    forward_head(1)
    forward_head(2)
    cacc[...] = jnp.zeros_like(cacc)
    zround(0, True)
    acopy.wait_recv()
    for way in range(2):
        start(zcopy(way, 0, None))
    wpartner(False)
    wnear(0)
    dproduct(0, 0)
    wrow()
    zround(1, True)
    wpartner(True)
    zround(0, False)
    dproduct(0, 1, -1)
    wnear(1)
    zround(2, True)
    pnear()
    dpass(0, 0)
    dpass(0, 1, -1)
    transposed(0)
    zround(1, False)
    dproduct(0, 2, -2)
    transposed(1)
    transposed(-1)
    tready()
    dproduct(1, 0, 1, -1)
    pfar()
    dpass(0, 2, -2)
    dpass(1, 0)
    dproduct(1, 2, -2)
    wfar()
    dpass(1, 1, -1)
    drelay(0, 0, 1, -1)
    transposed(2)
    transposed(-2)
    zround(2, False)
    dproduct(0, 3, -3)
    dpass(1, 2, -2)
    drelay(0, 2, -2)
    dproduct(1, 3, -3)
    drelay(1, 0, 1, -1)
    dpass(0, 3, -3)
    dpass(1, 3, -3)
    drelay(1, 2, -2)
    transposed(3)
    transposed(-3)
    prow()
    wdone(0)
    wdone(1)
    cproduct(1, range(-3, 4))
    zlast()
    transposed(4)
    dproduct(0, 4)
    cproduct(1, [4])
    for n in range(HEADS):
        csend[n] = cacc[1, :, pl.ds(n * HEAD_DIM, HEAD_DIM)].astype(BF)
        start(ccopy(n))
    dproduct(1, 4)
    dpass(0, 4)
    dpass(1, 4)
    cproduct(0, range(-3, 5))
    backward_head(0)
    backward_head(1)
    fs[0] = total(oyl, 0).astype(BF)
    start(ycopy(0))
    fs[1] = total(oyl, 1).astype(BF)
    start(ycopy(1))
    fs[2] = total(yl, 1).astype(BF)
    start(ycopy(2))
    backward_head(2)
    fkeep[...] = total(yl, 0)
    for i in range(3):
        ycopy(i).wait_recv()
    dw_ref[h] = fkeep[...] + yr[0].astype(F32)
    dw_ref[oh] = yr[1].astype(F32) + yr[2].astype(F32)

    for cp in sent:
        cp.wait_send()
    for s in range(4):
        for part in range(2):
            dcore(2 * s + oc, part).wait_send()
    for d in (0, 1, -1, 2, -2, 3, -3, 4):
        zp = zoff(d)
        for part in range(2):

            @pl.when(lax.rem(zp, 2) == c)
            def _():
                for yh in range(2):
                    xj, cp = dxcopy(zp, part, yh)

                    @pl.when(jnp.logical_not(even(zp)) if is_relayed(d) else xj != x)
                    def _():
                        cp.wait_send()

                if is_relayed(d):

                    @pl.when(even(zp))
                    def _():
                        for half in range(2):
                            dpcopy(zp, d, part, half).wait_send()


def shards(queries, keys, values, grad_out, out_weight):
    vmem = pl.BlockSpec(memory_space=pltpu.VMEM)
    hbm = pl.BlockSpec(memory_space=pltpu.HBM)
    dma = pltpu.SemaphoreType.DMA
    pairs = [
        (2, 12), (1,), (2,), (4, 2), (2, 3, 2), (8, 2),
        (3,), (3,), (4, 2), (5, 2, 2),
    ]
    sems = [dma((5,))]
    for shape in pairs:
        sems += [dma(shape), dma(shape)]
    sems += [dma((4, 2, 2)), dma((2, 3, 2)), dma((3,)), dma((3,))]
    block = pltpu.VMEM((SEQ, WIDTH), BF)
    operands = (queries, keys, values, grad_out, out_weight.reshape(2, HALF, WIDTH))
    operands = [pltpu.with_memory_space_constraint(a, pltpu.HBM) for a in operands]
    d_queries, d_keys, d_values, d_weight = pl.pallas_call(
        kernel,
        out_shape=(
            jax.ShapeDtypeStruct((SEQ, WIDTH), BF),
            jax.ShapeDtypeStruct((SEQ, WIDTH), BF),
            jax.ShapeDtypeStruct((SEQ, WIDTH), BF),
            jax.ShapeDtypeStruct((2, HALF, WIDTH), F32),
        ),
        in_specs=[hbm] * 5,
        out_specs=(vmem,) * 4,
        scratch_shapes=[
            block,
            block,
            block,
            block,
            pltpu.VMEM((2, HALF, WIDTH), BF),
            pltpu.VMEM((2, HALF, SEQ), BF),
            pltpu.VMEM((8, 2, HALF, SEQ), BF),
            pltpu.VMEM((8, SEQ, WIDTH), BF),
            pltpu.VMEM((8, 2, 2, HALF, WIDTH), BF),
            pltpu.VMEM((2 * HEADS, SEQ, HEAD_DIM), BF),
            pltpu.VMEM((HEADS, SEQ, SEQ), F32),
            pltpu.VMEM((2, SEQ, WIDTH), F32),
            pltpu.VMEM((HEADS, SEQ, HEAD_DIM), BF),
            pltpu.VMEM((HEADS, SEQ, HEAD_DIM), BF),
            block,
            pltpu.VMEM((8, 2, 2, HALF, WIDTH), BF),
            pltpu.VMEM((4, 2, 2, HALF, WIDTH), BF),
            pltpu.VMEM((5, 2, 2, HALF // 2, WIDTH), BF),
            pltpu.VMEM((2, 3, 2, HALF, WIDTH), BF),
            pltpu.VMEM((3, HALF, WIDTH), BF),
            pltpu.VMEM((3, HALF, WIDTH), BF),
            pltpu.VMEM((HALF, WIDTH), F32),
        ]
        + sems,
        compiler_params=pltpu.CompilerParams(
            collective_id=1, has_side_effects=True, vmem_limit_bytes=44 << 20
        ),
        cost_estimate=pl.CostEstimate(
            flops=6_000_000_000, bytes_accessed=4_000_000, transcendentals=800_000
        ),
    )(*operands)
    return d_queries, d_keys, d_values, d_weight.reshape(WIDTH, WIDTH)


def solution(mesh):
    placed = P("fsdp", "tensor")
    return jax.shard_map(
        shards,
        mesh=mesh,
        in_specs=(placed,) * 5,
        out_specs=(placed,) * 4,
        check_vma=False,
    )
```

```python
import functools

import jax
import jax.numpy as jnp
from jax import lax
from jax.experimental import pallas as pl
from jax.experimental.pallas import tpu as pltpu
from jax.sharding import PartitionSpec as P

HEAD_DIM = 128
SCALE = HEAD_DIM ** (-0.5)
MESH = pl.DeviceIdType.MESH
BF = jnp.bfloat16
F32 = jnp.float32
TN = (((0,), (0,)), ((), ()))
NT = (((1,), (1,)), ((), ()))

SEQ = 512
WIDTH = 384
HALF = 192
RELAYED = (0, 1, -1, 2, -2)
HEADS = 3
QCHUNK = 256


def dot(a, b):
    return jnp.dot(a, b, preferred_element_type=F32)


def dotg(a, b, dims):
    return lax.dot_general(a, b, dims, preferred_element_type=F32)


def kernel(
    q_hbm, k_hbm, v_hbm, g_hbm, w_hbm,
    dqkv_ref, dw_ref,
    q_ref, k_ref, v_ref, g_ref, w_ref,
    at, ag, an, wg, t2, probs, cacc, csend, crecv, gbuf, dall, dr, xp, xr, fs, yr, fkeep,
    in_s,
    z_s, z_r, a_s, a_r, wp_s, wp_r, wy_s, wy_r, wx_s, wx_r, wc_s, wc_r,
    t_s, t_r, c_s, c_r, dc_s, dc_r, dp_s, dp_r, dx_s, dx_r, dy_s, dy_r,
):
    f = lax.axis_index("fsdp")
    t = lax.axis_index("tensor")
    x = lax.div(f, 4)
    yl = lax.rem(lax.div(f, 2), 2)
    c = lax.rem(f, 2)
    h = lax.div(t, 8)
    z = lax.rem(t, 8)
    oh = 1 - h
    oyl = 1 - yl
    oc = 1 - c

    def dev(x_=None, yl_=None, c_=None, h_=None, z_=None):
        x_ = x if x_ is None else x_
        yl_ = yl if yl_ is None else yl_
        c_ = c if c_ is None else c_
        h_ = h if h_ is None else h_
        z_ = z if z_ is None else z_
        return (x_ * 4 + yl_ * 2 + c_, h_ * 8 + z_)

    def zoff(d):
        return lax.rem(z + 8 + d, 8)

    def xoff(d):
        return lax.rem(x + 4 + d, 4)

    def rcopy(src, dst, ssem, rsem, device):
        return pltpu.make_async_remote_copy(
            src_ref=src, dst_ref=dst, send_sem=ssem, recv_sem=rsem,
            device_id=device, device_id_type=MESH,
        )

    loads = {}
    for i, (name, src, dst) in enumerate((
        ("g", g_hbm, g_ref), ("w", w_hbm, w_ref), ("k", k_hbm, k_ref),
        ("q", q_hbm, q_ref), ("v", v_hbm, v_ref),
    )):
        loads[name] = pltpu.make_async_copy(src, dst, in_s.at[i])
        loads[name].start()

    peers = [
        dev(z_=zoff(1)), dev(z_=zoff(-1)),
        dev(h_=oh), dev(yl_=oyl), dev(yl_=oyl, h_=oh),
        dev(x_=xoff(1)), dev(x_=xoff(-1)), dev(x_=xoff(2)),
        dev(c_=oc),
    ]
    barrier = pltpu.get_barrier_semaphore()
    for peer in peers:
        pl.semaphore_signal(barrier, inc=1, device_id=peer, device_id_type=MESH)

    sent = []

    def start(cp):
        cp.start()
        sent.append(cp)

    def zcopy(way, k, half):
        src = zoff(-k) if way == 0 else zoff(k)
        to = dev(z_=zoff(1)) if way == 0 else dev(z_=zoff(-1))
        if half is None:
            i = 8 + k
            ref = ag.at[src, oh]
        else:
            i = 2 * k + half
            ref = ag.at[src, h, pl.ds(half * (HALF // 2), HALF // 2)]
        return rcopy(ref, ref, z_s.at[way, i], z_r.at[way, i], to)

    def wblock(x_, yl_, part):
        return wg.at[lax.rem(x_, 2) * 4 + yl_ * 2 + c, part, lax.div(x_, 2)]

    def wycopy(d, part):
        ref = wblock(xoff(d), yl, part)
        return rcopy(ref, ref, wy_s.at[d, part], wy_r.at[d, part], dev(yl_=oyl))

    def wpcopy(same_row):
        i = 0 if same_row else 1
        to = dev(h_=oh) if same_row else dev(yl_=oyl, h_=oh)
        return rcopy(w_ref.at[oh], wblock(x, yl, 1), wp_s.at[i], wp_r.at[i], to)

    def wxcopy(way, i, part):
        to = dev(x_=xoff(1)) if way == 0 else dev(x_=xoff(-1))
        if i == 0:
            ref = wblock(x, yl, part)
        elif i == 1:
            ref = wblock(x, oyl, part)
        elif part == 0:
            ref = wblock(xoff(-1), yl, part) if way == 0 else wblock(xoff(1), oyl, part)
        else:
            ref = wblock(xoff(-1 if way == 0 else 1), yl, part)
            ref = ref.at[pl.ds(way * (HALF // 2), HALF // 2)]
        return rcopy(ref, ref, wx_s.at[way, i, part], wx_r.at[way, i, part], to)

    def wccopy(d, own_row, part):
        ref = wblock(xoff(d), yl if own_row else oyl, part)
        i = 2 * d + (0 if own_row else 1)
        return rcopy(ref, ref, wc_s.at[i, part], wc_r.at[i, part], dev(c_=oc))

    def tcopy(n):
        return rcopy(t2.at[n], t2.at[HEADS + n], t_s.at[n], t_r.at[n], dev(h_=oh))

    def ccopy(n):
        return rcopy(csend.at[n], crecv.at[n], c_s.at[n], c_r.at[n], dev(h_=oh))

    def forward_head(n):
        cols = slice(n * HEAD_DIM, (n + 1) * HEAD_DIM)
        for i in range(SEQ // QCHUNK):
            rows = slice(i * QCHUNK, (i + 1) * QCHUNK)
            st = dotg(k_ref[:, cols], q_ref[rows, cols], NT) * SCALE
            e = jnp.exp(st - jnp.max(st, axis=0, keepdims=True))
            p = e * (1.0 / jnp.sum(e, axis=0, keepdims=True))
            probs[n, :, rows] = p
            t2[n, rows] = dotg(p.astype(BF), v_ref[:, cols], TN).astype(BF)
        start(tcopy(n))

    def backward_head(n):
        cols = slice(n * HEAD_DIM, (n + 1) * HEAD_DIM)
        ccopy(n).wait_recv()
        gbuf[:, cols] = (cacc[0, :, cols] + crecv[n].astype(F32)).astype(BF)
        dk = jnp.zeros((SEQ, HEAD_DIM), F32)
        dv = jnp.zeros((SEQ, HEAD_DIM), F32)
        for i in range(SEQ // QCHUNK):
            rows = slice(i * QCHUNK, (i + 1) * QCHUNK)
            p = probs[n, :, rows]
            gh = gbuf[rows, cols]
            gp = dotg(v_ref[:, cols], gh, NT)
            rd = jnp.sum(p * gp, axis=0, keepdims=True)
            ds = (p * (gp - rd) * SCALE).astype(BF)
            dqkv_ref[0, rows, cols] = dotg(ds, k_ref[:, cols], TN).astype(BF)
            dk = dk + dot(ds, q_ref[rows, cols])
            dv = dv + dot(p.astype(BF), gh)
        dqkv_ref[1, :, cols] = dk.astype(BF)
        dqkv_ref[2, :, cols] = dv.astype(BF)

    def dcore(zp, part):
        s = lax.div(zp, 2)
        return rcopy(
            dall.at[zp, part], dr.at[s, part], dc_s.at[s, part], dc_r.at[s, part], dev(c_=oc)
        )

    def dxcopy(zp, part, yh):
        s = lax.div(zp, 2)
        xj = 2 * yh + lax.div(zp, 4)
        row = lax.rem(s, 2)
        slot = lax.max(lax.rem(x - xj + 4, 4) - 1, 0)
        return xj, rcopy(
            dall.at[zp, part, yh], xr.at[row, slot, part],
            dx_s.at[s, part, yh], dx_r.at[row, slot, part], dev(x_=xj),
        )

    def dproduct(part, *ds):
        b = jnp.concatenate([t2[part * HEADS + n] for n in range(HEADS)], axis=1)
        for d in ds:
            zp = zoff(d)
            for yh in range(2):
                dall[zp, part, yh] = dot(ag[zp, yh], b).astype(BF)

            @pl.when(lax.rem(zp, 2) != c)
            def _():
                dcore(zp, part).start()

    def even(zp):
        return lax.rem(x, 2) == lax.div(zp, 4)

    def is_relayed(d):
        return d in RELAYED

    def dpcopy(zp, d, part, half):
        i = RELAYED.index(d)
        src = dall.at[zp, part, 1 - lax.div(x, 2), pl.ds(half * (HALF // 2), HALF // 2)]
        to = dev(x_=xoff(-1)) if half == 0 else dev(x_=xoff(1))
        return rcopy(
            src, xp.at[i, part, half], dp_s.at[i, part, half], dp_r.at[i, part, half], to
        )

    def dpass(part, *ds):
        for d in ds:
            zp = zoff(d)

            @pl.when(lax.rem(zp, 2) == c)
            def _():
                s = lax.div(zp, 2)
                dcore(zp, part).wait_recv()
                for yh in range(2):
                    dall[zp, part, yh] = (
                        dall[zp, part, yh].astype(F32) + dr[s, part, yh].astype(F32)
                    ).astype(BF)
                    if not is_relayed(d):
                        xj, cp = dxcopy(zp, part, yh)

                        @pl.when(xj != x)
                        def _():
                            cp.start()

                if is_relayed(d):

                    @pl.when(even(zp))
                    def _():
                        for half in range(2):
                            dpcopy(zp, d, part, half).start()

    def drelay(part, *ds):
        for d in ds:
            zp = zoff(d)

            @pl.when((lax.rem(zp, 2) == c) & jnp.logical_not(even(zp)))
            def _():
                for half in range(2):
                    dpcopy(zp, d, part, half).wait_recv()
                    yh = lax.div(xoff(-1) if half == 0 else xoff(1), 2)
                    rows = pl.ds(half * (HALF // 2), HALF // 2)
                    dall[zp, part, yh, rows] = (
                        dall[zp, part, yh, rows].astype(F32)
                        + xp[RELAYED.index(d), part, half].astype(F32)
                    ).astype(BF)
                    dxcopy(zp, part, yh)[1].start()

    def total(row, part):
        zf = lax.rem(x, 2) * 4 + row * 2 + c
        yh = lax.div(x, 2)
        away = lax.rem(zf - z + 8, 8)
        relayed = (away <= 2) | (away >= 6)
        for i in range(3):
            arrival = rcopy(
                xr.at[row, i, part], xr.at[row, i, part], dx_s.at[0, 0, 0],
                dx_r.at[row, i, part], dev(x_=xoff(1)),
            )
            if i == 1:

                @pl.when(jnp.logical_not(relayed))
                def _():
                    arrival.wait_recv()

                @pl.when(relayed)
                def _():
                    xr[row, 1, part] = jnp.zeros((HALF, WIDTH), BF)

            else:
                arrival.wait_recv()
        acc = dall[zf, part, yh].astype(F32)
        for i in range(3):
            acc = acc + xr[row, i, part].astype(F32)
        return acc

    def ycopy(i):
        to = (dev(yl_=oyl), dev(yl_=oyl, h_=oh), dev(h_=oh))[i]
        return rcopy(fs.at[i], yr.at[i], dy_s.at[i], dy_r.at[i], to)

    def transposed(d):
        zp = zoff(d)
        an[zp] = ag[zp].reshape(WIDTH, SEQ).T

    def cproduct(part, ds):
        for i in range(2):
            rows = slice(i * 256, (i + 1) * 256)
            acc = cacc[part, rows]
            for d in ds:
                zp = zoff(d)
                acc = acc + dot(an[zp, rows], wg[zp, part].reshape(WIDTH, WIDTH))
            cacc[part, rows] = acc

    def zround(k, own):
        for half in (0, 1) if own else (None,):
            for way in range(2):
                zcopy(way, k, half).wait_recv()
                if k < 2 or (way == 0) == own:
                    start(zcopy(way, k + 1, half))

    def wsend(own_row, part):
        for way in range(2):
            start(wxcopy(way, 0 if own_row else 1, part))
        start(wccopy(0, own_row, part))

    def wrow():
        wycopy(0, 0).wait_recv()
        wsend(False, 0)

    def wpartner(same_row):
        wpcopy(same_row).wait_recv()
        if same_row:
            wsend(True, 1)
        else:
            start(wccopy(0, False, 1))

    def wnear(i):
        for way, d in ((0, 3), (1, 1)):
            wxcopy(way, i, 0).wait_recv()
            if way == i:
                start(wxcopy(way, 2, 0))
            start(wccopy(d, i == 0, 0))

    def wfar():
        for way in range(2):
            wxcopy(way, 2, 0).wait_recv()
            start(wccopy(2, way == 0, 0))

    def pnear():
        for way, d in ((0, 3), (1, 1)):
            wxcopy(way, 0, 1).wait_recv()
            start(wxcopy(way, 2, 1))
            start(wycopy(d, 1))
            start(wccopy(d, True, 1))

    def pfar():
        for way in range(2):
            wxcopy(way, 2, 1).wait_recv()
        start(wycopy(2, 1))
        start(wccopy(2, True, 1))

    def prow():
        for d in (3, 1, 2):
            wycopy(d, 1).wait_recv()
            start(wccopy(d, False, 1))

    def tready():
        for n in range(HEADS):
            tcopy(n).wait_recv()

    def wdone(part):
        for d in range(4):
            for own_row in (True, False):
                wccopy(d, own_row, part).wait_recv()

    def zlast():
        zcopy(0, 3, 0).wait_recv()
        zcopy(0, 3, 1).wait_recv()
        zcopy(1, 3, None).wait_recv()

    zj = lax.rem(x, 2) * 4 + yl * 2 + c
    yj = lax.div(x, 2)
    loads["g"].wait()
    at[...] = g_ref[...].T.reshape(2, HALF, SEQ)
    ag[z, h] = at[h]
    loads["w"].wait()
    wg[zj, 0, yj] = w_ref[h]
    pl.semaphore_wait(barrier, len(peers))

    acopy = rcopy(at.at[oh], ag.at[z, h], a_s.at[0], a_r.at[0], dev(h_=oh))
    start(acopy)
    for half in range(2):
        for way in range(2):
            start(zcopy(way, 0, half))
    for way in range(2):
        start(wxcopy(way, 0, 0))
    start(wycopy(0, 0))
    start(wpcopy(False))
    start(wpcopy(True))
    start(wccopy(0, True, 0))

    for name in ("k", "q", "v"):
        loads[name].wait()
    forward_head(0)
    forward_head(1)
    forward_head(2)
    cacc[...] = jnp.zeros_like(cacc)
    zround(0, True)
    acopy.wait_recv()
    for way in range(2):
        start(zcopy(way, 0, None))
    wpartner(False)
    wnear(0)
    dproduct(0, 0)
    wrow()
    zround(1, True)
    wpartner(True)
    zround(0, False)
    dproduct(0, 1, -1)
    wnear(1)
    zround(2, True)
    pnear()
    dpass(0, 0)
    dpass(0, 1, -1)
    transposed(0)
    zround(1, False)
    dproduct(0, 2, -2)
    transposed(1)
    transposed(-1)
    tready()
    dproduct(1, 0, 1, -1)
    pfar()
    dpass(0, 2, -2)
    dpass(1, 0)
    dproduct(1, 2, -2)
    wfar()
    dpass(1, 1, -1)
    drelay(0, 0, 1, -1)
    transposed(2)
    transposed(-2)
    zround(2, False)
    dproduct(0, 3, -3)
    dpass(1, 2, -2)
    drelay(0, 2, -2)
    dproduct(1, 3, -3)
    drelay(1, 0, 1, -1)
    dpass(0, 3, -3)
    dpass(1, 3, -3)
    drelay(1, 2, -2)
    transposed(3)
    transposed(-3)
    prow()
    wdone(0)
    wdone(1)
    cproduct(1, range(-3, 4))
    zlast()
    transposed(4)
    dproduct(0, 4)
    cproduct(1, [4])
    for n in range(HEADS):
        csend[n] = cacc[1, :, pl.ds(n * HEAD_DIM, HEAD_DIM)].astype(BF)
        start(ccopy(n))
    dproduct(1, 4)
    dpass(0, 4)
    dpass(1, 4)
    cproduct(0, range(-3, 5))
    backward_head(0)
    backward_head(1)
    fs[0] = total(oyl, 0).astype(BF)
    start(ycopy(0))
    fs[1] = total(oyl, 1).astype(BF)
    start(ycopy(1))
    fs[2] = total(yl, 1).astype(BF)
    start(ycopy(2))
    backward_head(2)
    fkeep[...] = total(yl, 0)
    for i in range(3):
        ycopy(i).wait_recv()
    dw_ref[h] = fkeep[...] + yr[0].astype(F32)
    dw_ref[oh] = yr[1].astype(F32) + yr[2].astype(F32)

    for cp in sent:
        cp.wait_send()
    for s in range(4):
        for part in range(2):
            dcore(2 * s + oc, part).wait_send()
    for d in (0, 1, -1, 2, -2, 3, -3, 4):
        zp = zoff(d)
        for part in range(2):

            @pl.when(lax.rem(zp, 2) == c)
            def _():
                for yh in range(2):
                    xj, cp = dxcopy(zp, part, yh)

                    @pl.when(jnp.logical_not(even(zp)) if is_relayed(d) else xj != x)
                    def _():
                        cp.wait_send()

                if is_relayed(d):

                    @pl.when(even(zp))
                    def _():
                        for half in range(2):
                            dpcopy(zp, d, part, half).wait_send()


def shards(queries, keys, values, grad_out, out_weight):
    vmem = pl.BlockSpec(memory_space=pltpu.VMEM)
    hbm = pl.BlockSpec(memory_space=pltpu.HBM)
    dma = pltpu.SemaphoreType.DMA
    pairs = [
        (2, 12), (1,), (2,), (4, 2), (2, 3, 2), (8, 2),
        (3,), (3,), (4, 2), (5, 2, 2),
    ]
    sems = [dma((5,))]
    for shape in pairs:
        sems += [dma(shape), dma(shape)]
    sems += [dma((4, 2, 2)), dma((2, 3, 2)), dma((3,)), dma((3,))]
    block = pltpu.VMEM((SEQ, WIDTH), BF)
    operands = (queries, keys, values, grad_out, out_weight.reshape(2, HALF, WIDTH))
    operands = [pltpu.with_memory_space_constraint(a, pltpu.HBM) for a in operands]
    d_attention, d_weight = pl.pallas_call(
        kernel,
        out_shape=(
            jax.ShapeDtypeStruct((3, SEQ, WIDTH), BF),
            jax.ShapeDtypeStruct((2, HALF, WIDTH), F32),
        ),
        in_specs=[hbm] * 5,
        out_specs=(vmem,) * 2,
        scratch_shapes=[
            block,
            block,
            block,
            block,
            pltpu.VMEM((2, HALF, WIDTH), BF),
            pltpu.VMEM((2, HALF, SEQ), BF),
            pltpu.VMEM((8, 2, HALF, SEQ), BF),
            pltpu.VMEM((8, SEQ, WIDTH), BF),
            pltpu.VMEM((8, 2, 2, HALF, WIDTH), BF),
            pltpu.VMEM((2 * HEADS, SEQ, HEAD_DIM), BF),
            pltpu.VMEM((HEADS, SEQ, SEQ), F32),
            pltpu.VMEM((2, SEQ, WIDTH), F32),
            pltpu.VMEM((HEADS, SEQ, HEAD_DIM), BF),
            pltpu.VMEM((HEADS, SEQ, HEAD_DIM), BF),
            block,
            pltpu.VMEM((8, 2, 2, HALF, WIDTH), BF),
            pltpu.VMEM((4, 2, 2, HALF, WIDTH), BF),
            pltpu.VMEM((5, 2, 2, HALF // 2, WIDTH), BF),
            pltpu.VMEM((2, 3, 2, HALF, WIDTH), BF),
            pltpu.VMEM((3, HALF, WIDTH), BF),
            pltpu.VMEM((3, HALF, WIDTH), BF),
            pltpu.VMEM((HALF, WIDTH), F32),
        ]
        + sems,
        compiler_params=pltpu.CompilerParams(
            collective_id=1, has_side_effects=True, vmem_limit_bytes=44 << 20
        ),
        cost_estimate=pl.CostEstimate(
            flops=6_000_000_000, bytes_accessed=4_000_000, transcendentals=800_000
        ),
    )(*operands)
    return d_attention[0], d_attention[1], d_attention[2], d_weight.reshape(WIDTH, WIDTH)


def solution(mesh):
    placed = P("fsdp", "tensor")
    return jax.shard_map(
        shards,
        mesh=mesh,
        in_specs=(placed,) * 5,
        out_specs=(placed,) * 4,
        check_vma=False,
    )
```

```python
import functools

import jax
import jax.numpy as jnp
from jax import lax
from jax.experimental import pallas as pl
from jax.experimental.pallas import tpu as pltpu
from jax.sharding import PartitionSpec as P

HEAD_DIM = 128
SCALE = HEAD_DIM ** (-0.5)
MESH = pl.DeviceIdType.MESH
BF = jnp.bfloat16
F32 = jnp.float32
TN = (((0,), (0,)), ((), ()))
NT = (((1,), (1,)), ((), ()))

SEQ = 512
WIDTH = 384
HALF = 192
RELAYED = (0, 1, -1, 2, -2)
HEADS = 3
QCHUNK = 256


def dot(a, b):
    return jnp.dot(a, b, preferred_element_type=F32)


def dotg(a, b, dims):
    return lax.dot_general(a, b, dims, preferred_element_type=F32)


def kernel(
    q_hbm, k_hbm, v_hbm, g_hbm, w_hbm,
    dqkv_ref, dw_ref,
    q_ref, k_ref, v_ref, g_ref, w_ref,
    at, ag, an, wg, t2, probs, cacc, csend, crecv, gbuf, dall, dr, xp, xr, fs, yr, fkeep,
    in_s,
    z_s, z_r, a_s, a_r, wp_s, wp_r, wy_s, wy_r, wx_s, wx_r, wc_s, wc_r,
    t_s, t_r, c_s, c_r, dc_s, dc_r, dp_s, dp_r, dx_s, dx_r, dy_s, dy_r,
):
    f = lax.axis_index("fsdp")
    t = lax.axis_index("tensor")
    x = lax.div(f, 4)
    yl = lax.rem(lax.div(f, 2), 2)
    c = lax.rem(f, 2)
    h = lax.div(t, 8)
    z = lax.rem(t, 8)
    oh = 1 - h
    oyl = 1 - yl
    oc = 1 - c

    def dev(x_=None, yl_=None, c_=None, h_=None, z_=None):
        x_ = x if x_ is None else x_
        yl_ = yl if yl_ is None else yl_
        c_ = c if c_ is None else c_
        h_ = h if h_ is None else h_
        z_ = z if z_ is None else z_
        return (x_ * 4 + yl_ * 2 + c_, h_ * 8 + z_)

    def zoff(d):
        return lax.rem(z + 8 + d, 8)

    def xoff(d):
        return lax.rem(x + 4 + d, 4)

    def rcopy(src, dst, ssem, rsem, device):
        return pltpu.make_async_remote_copy(
            src_ref=src, dst_ref=dst, send_sem=ssem, recv_sem=rsem,
            device_id=device, device_id_type=MESH,
        )

    loads = {}
    for i, (name, src, dst) in enumerate((
        ("g", g_hbm, g_ref), ("w", w_hbm, w_ref), ("k", k_hbm, k_ref),
        ("q", q_hbm, q_ref), ("v", v_hbm, v_ref),
    )):
        loads[name] = pltpu.make_async_copy(src, dst, in_s.at[i])
        loads[name].start()

    peers = [
        dev(z_=zoff(1)), dev(z_=zoff(-1)),
        dev(h_=oh), dev(yl_=oyl), dev(yl_=oyl, h_=oh),
        dev(x_=xoff(1)), dev(x_=xoff(-1)), dev(x_=xoff(2)),
        dev(c_=oc),
    ]
    barrier = pltpu.get_barrier_semaphore()
    for peer in peers:
        pl.semaphore_signal(barrier, inc=1, device_id=peer, device_id_type=MESH)

    sent = []

    def start(cp):
        cp.start()
        sent.append(cp)

    def zcopy(way, k, half):
        src = zoff(-k) if way == 0 else zoff(k)
        to = dev(z_=zoff(1)) if way == 0 else dev(z_=zoff(-1))
        if half is None:
            i = 8 + k
            ref = ag.at[src, oh]
        else:
            i = 2 * k + half
            ref = ag.at[src, h, pl.ds(half * (HALF // 2), HALF // 2)]
        return rcopy(ref, ref, z_s.at[way, i], z_r.at[way, i], to)

    def wblock(x_, yl_, part):
        return wg.at[lax.rem(x_, 2) * 4 + yl_ * 2 + c, part, lax.div(x_, 2)]

    def wycopy(d, part):
        ref = wblock(xoff(d), yl, part)
        return rcopy(ref, ref, wy_s.at[d, part], wy_r.at[d, part], dev(yl_=oyl))

    def wpcopy(same_row):
        i = 0 if same_row else 1
        to = dev(h_=oh) if same_row else dev(yl_=oyl, h_=oh)
        return rcopy(w_ref.at[oh], wblock(x, yl, 1), wp_s.at[i], wp_r.at[i], to)

    def wxcopy(way, i, part):
        to = dev(x_=xoff(1)) if way == 0 else dev(x_=xoff(-1))
        if i == 0:
            ref = wblock(x, yl, part)
        elif i == 1:
            ref = wblock(x, oyl, part)
        elif part == 0:
            ref = wblock(xoff(-1), yl, part) if way == 0 else wblock(xoff(1), oyl, part)
        else:
            ref = wblock(xoff(-1 if way == 0 else 1), yl, part)
            ref = ref.at[pl.ds(way * (HALF // 2), HALF // 2)]
        return rcopy(ref, ref, wx_s.at[way, i, part], wx_r.at[way, i, part], to)

    def wccopy(d, own_row, part):
        ref = wblock(xoff(d), yl if own_row else oyl, part)
        i = 2 * d + (0 if own_row else 1)
        return rcopy(ref, ref, wc_s.at[i, part], wc_r.at[i, part], dev(c_=oc))

    def tcopy(n):
        return rcopy(t2.at[n], t2.at[HEADS + n], t_s.at[n], t_r.at[n], dev(h_=oh))

    def ccopy(n):
        return rcopy(csend.at[n], crecv.at[n], c_s.at[n], c_r.at[n], dev(h_=oh))

    def forward_head(n):
        cols = slice(n * HEAD_DIM, (n + 1) * HEAD_DIM)
        for i in range(SEQ // QCHUNK):
            rows = slice(i * QCHUNK, (i + 1) * QCHUNK)
            st = dotg(k_ref[:, cols], q_ref[rows, cols], NT) * SCALE
            e = jnp.exp(st - jnp.max(st, axis=0, keepdims=True))
            p = e * (1.0 / jnp.sum(e, axis=0, keepdims=True))
            probs[n, :, rows] = p
            t2[n, rows] = dotg(p.astype(BF), v_ref[:, cols], TN).astype(BF)
        start(tcopy(n))

    def backward_head(n):
        cols = slice(n * HEAD_DIM, (n + 1) * HEAD_DIM)
        ccopy(n).wait_recv()
        gbuf[:, cols] = (cacc[0, :, cols] + crecv[n].astype(F32)).astype(BF)
        dk = jnp.zeros((SEQ, HEAD_DIM), F32)
        dv = jnp.zeros((SEQ, HEAD_DIM), F32)
        for i in range(SEQ // QCHUNK):
            rows = slice(i * QCHUNK, (i + 1) * QCHUNK)
            p = probs[n, :, rows]
            gh = gbuf[rows, cols]
            gp = dotg(v_ref[:, cols], gh, NT)
            rd = jnp.sum(p * gp, axis=0, keepdims=True)
            ds = (p * (gp - rd) * SCALE).astype(BF)
            dqkv_ref[0, rows, cols] = dotg(ds, k_ref[:, cols], TN).astype(BF)
            dk = dk + dot(ds, q_ref[rows, cols])
            dv = dv + dot(p.astype(BF), gh)
        dqkv_ref[1, :, cols] = dk.astype(BF)
        dqkv_ref[2, :, cols] = dv.astype(BF)

    def dcore(zp, part):
        s = lax.div(zp, 2)
        return rcopy(
            dall.at[zp, part], dr.at[s, part], dc_s.at[s, part], dc_r.at[s, part], dev(c_=oc)
        )

    def dxcopy(zp, part, yh):
        s = lax.div(zp, 2)
        xj = 2 * yh + lax.div(zp, 4)
        row = lax.rem(s, 2)
        slot = lax.max(lax.rem(x - xj + 4, 4) - 1, 0)
        return xj, rcopy(
            dall.at[zp, part, yh], xr.at[row, slot, part],
            dx_s.at[s, part, yh], dx_r.at[row, slot, part], dev(x_=xj),
        )

    def dproduct(part, *ds):
        b = jnp.concatenate([t2[part * HEADS + n] for n in range(HEADS)], axis=1)
        for d in ds:
            zp = zoff(d)
            for yh in range(2):
                dall[zp, part, yh] = dot(ag[zp, yh], b).astype(BF)

            @pl.when(lax.rem(zp, 2) != c)
            def _():
                dcore(zp, part).start()

    def even(zp):
        return lax.rem(x, 2) == lax.div(zp, 4)

    def is_relayed(d):
        return d in RELAYED

    def dpcopy(zp, d, part, half):
        i = RELAYED.index(d)
        src = dall.at[zp, part, 1 - lax.div(x, 2), pl.ds(half * (HALF // 2), HALF // 2)]
        to = dev(x_=xoff(-1)) if half == 0 else dev(x_=xoff(1))
        return rcopy(
            src, xp.at[i, part, half], dp_s.at[i, part, half], dp_r.at[i, part, half], to
        )

    def dpass(part, *ds):
        for d in ds:
            zp = zoff(d)

            @pl.when(lax.rem(zp, 2) == c)
            def _():
                s = lax.div(zp, 2)
                dcore(zp, part).wait_recv()
                for yh in range(2):
                    dall[zp, part, yh] = (
                        dall[zp, part, yh].astype(F32) + dr[s, part, yh].astype(F32)
                    ).astype(BF)
                    if not is_relayed(d):
                        xj, cp = dxcopy(zp, part, yh)

                        @pl.when(xj != x)
                        def _():
                            cp.start()

                if is_relayed(d):

                    @pl.when(even(zp))
                    def _():
                        for half in range(2):
                            dpcopy(zp, d, part, half).start()

    def drelay(part, *ds):
        for d in ds:
            zp = zoff(d)

            @pl.when((lax.rem(zp, 2) == c) & jnp.logical_not(even(zp)))
            def _():
                for half in range(2):
                    dpcopy(zp, d, part, half).wait_recv()
                    yh = lax.div(xoff(-1) if half == 0 else xoff(1), 2)
                    rows = pl.ds(half * (HALF // 2), HALF // 2)
                    dall[zp, part, yh, rows] = (
                        dall[zp, part, yh, rows].astype(F32)
                        + xp[RELAYED.index(d), part, half].astype(F32)
                    ).astype(BF)
                    dxcopy(zp, part, yh)[1].start()

    def total(row, part):
        zf = lax.rem(x, 2) * 4 + row * 2 + c
        yh = lax.div(x, 2)
        away = lax.rem(zf - z + 8, 8)
        relayed = (away <= 2) | (away >= 6)
        for i in range(3):
            arrival = rcopy(
                xr.at[row, i, part], xr.at[row, i, part], dx_s.at[0, 0, 0],
                dx_r.at[row, i, part], dev(x_=xoff(1)),
            )
            if i == 1:

                @pl.when(jnp.logical_not(relayed))
                def _():
                    arrival.wait_recv()

                @pl.when(relayed)
                def _():
                    xr[row, 1, part] = jnp.zeros((HALF, WIDTH), BF)

            else:
                arrival.wait_recv()
        acc = dall[zf, part, yh].astype(F32)
        for i in range(3):
            acc = acc + xr[row, i, part].astype(F32)
        return acc

    def ycopy(i):
        to = (dev(yl_=oyl), dev(yl_=oyl, h_=oh), dev(h_=oh))[i]
        return rcopy(fs.at[i], yr.at[i], dy_s.at[i], dy_r.at[i], to)

    def transposed(d):
        zp = zoff(d)
        an[zp] = ag[zp].reshape(WIDTH, SEQ).T

    def cproduct(part, ds):
        for i in range(2):
            rows = slice(i * 256, (i + 1) * 256)
            acc = cacc[part, rows]
            for d in ds:
                zp = zoff(d)
                acc = acc + dot(an[zp, rows], wg[zp, part].reshape(WIDTH, WIDTH))
            cacc[part, rows] = acc

    def zround(k, own):
        for half in (0, 1) if own else (None,):
            for way in range(2):
                zcopy(way, k, half).wait_recv()
                if k < 2 or (way == 0) == own:
                    start(zcopy(way, k + 1, half))

    def wsend(own_row, part):
        for way in range(2):
            start(wxcopy(way, 0 if own_row else 1, part))
        start(wccopy(0, own_row, part))

    def wrow():
        wycopy(0, 0).wait_recv()
        wsend(False, 0)

    def wpartner(same_row):
        wpcopy(same_row).wait_recv()
        if same_row:
            wsend(True, 1)
        else:
            start(wccopy(0, False, 1))

    def wnear(i):
        for way, d in ((0, 3), (1, 1)):
            wxcopy(way, i, 0).wait_recv()
            if way == i:
                start(wxcopy(way, 2, 0))
            start(wccopy(d, i == 0, 0))

    def wfar():
        for way in range(2):
            wxcopy(way, 2, 0).wait_recv()
            start(wccopy(2, way == 0, 0))

    def pnear():
        for way, d in ((0, 3), (1, 1)):
            wxcopy(way, 0, 1).wait_recv()
            start(wxcopy(way, 2, 1))
            start(wycopy(d, 1))
            start(wccopy(d, True, 1))

    def pfar():
        for way in range(2):
            wxcopy(way, 2, 1).wait_recv()
        start(wycopy(2, 1))
        start(wccopy(2, True, 1))

    def prow():
        for d in (3, 1, 2):
            wycopy(d, 1).wait_recv()
            start(wccopy(d, False, 1))

    def tready():
        for n in range(HEADS):
            tcopy(n).wait_recv()

    def wdone(part):
        for d in range(4):
            for own_row in (True, False):
                wccopy(d, own_row, part).wait_recv()

    def zlast():
        zcopy(0, 3, 0).wait_recv()
        zcopy(0, 3, 1).wait_recv()
        zcopy(1, 3, None).wait_recv()

    zj = lax.rem(x, 2) * 4 + yl * 2 + c
    yj = lax.div(x, 2)
    loads["g"].wait()
    at[...] = g_ref[...].T.reshape(2, HALF, SEQ)
    ag[z, h] = at[h]
    loads["w"].wait()
    wg[zj, 0, yj] = w_ref[h]
    pl.semaphore_wait(barrier, len(peers))

    acopy = rcopy(at.at[oh], ag.at[z, h], a_s.at[0], a_r.at[0], dev(h_=oh))
    start(acopy)
    for half in range(2):
        for way in range(2):
            start(zcopy(way, 0, half))
    for way in range(2):
        start(wxcopy(way, 0, 0))
    start(wycopy(0, 0))
    start(wpcopy(False))
    start(wpcopy(True))
    start(wccopy(0, True, 0))

    for name in ("k", "q", "v"):
        loads[name].wait()
    forward_head(0)
    forward_head(1)
    forward_head(2)
    cacc[...] = jnp.zeros_like(cacc)
    zround(0, True)
    acopy.wait_recv()
    for way in range(2):
        start(zcopy(way, 0, None))
    wpartner(False)
    wnear(0)
    dproduct(0, 0)
    wrow()
    zround(1, True)
    wpartner(True)
    zround(0, False)
    dproduct(0, 1, -1)
    wnear(1)
    zround(2, True)
    pnear()
    dpass(0, 0)
    dpass(0, 1, -1)
    transposed(0)
    zround(1, False)
    dproduct(0, 2, -2)
    transposed(1)
    transposed(-1)
    tready()
    dproduct(1, 0, 1, -1)
    pfar()
    dpass(0, 2, -2)
    dpass(1, 0)
    dproduct(1, 2, -2)
    wfar()
    dpass(1, 1, -1)
    drelay(0, 0, 1, -1)
    transposed(2)
    transposed(-2)
    zround(2, False)
    dproduct(0, 3, -3)
    dpass(1, 2, -2)
    drelay(0, 2, -2)
    dproduct(1, 3, -3)
    drelay(1, 0, 1, -1)
    dpass(0, 3, -3)
    dpass(1, 3, -3)
    drelay(1, 2, -2)
    transposed(3)
    transposed(-3)
    prow()
    wdone(0)
    wdone(1)
    cproduct(1, range(-3, 4))
    zlast()
    transposed(4)
    dproduct(0, 4)
    cproduct(1, [4])
    for n in range(HEADS):
        csend[n] = cacc[1, :, pl.ds(n * HEAD_DIM, HEAD_DIM)].astype(BF)
        start(ccopy(n))
    dproduct(1, 4)
    dpass(0, 4)
    dpass(1, 4)
    cproduct(0, range(-3, 5))
    backward_head(0)
    fs[0] = total(oyl, 0).astype(BF)
    start(ycopy(0))
    fs[1] = total(oyl, 1).astype(BF)
    start(ycopy(1))
    fs[2] = total(yl, 1).astype(BF)
    start(ycopy(2))
    backward_head(1)
    backward_head(2)
    fkeep[...] = total(yl, 0)
    for i in range(3):
        ycopy(i).wait_recv()
    dw_ref[h] = fkeep[...] + yr[0].astype(F32)
    dw_ref[oh] = yr[1].astype(F32) + yr[2].astype(F32)

    for cp in sent:
        cp.wait_send()
    for s in range(4):
        for part in range(2):
            dcore(2 * s + oc, part).wait_send()
    for d in (0, 1, -1, 2, -2, 3, -3, 4):
        zp = zoff(d)
        for part in range(2):

            @pl.when(lax.rem(zp, 2) == c)
            def _():
                for yh in range(2):
                    xj, cp = dxcopy(zp, part, yh)

                    @pl.when(jnp.logical_not(even(zp)) if is_relayed(d) else xj != x)
                    def _():
                        cp.wait_send()

                if is_relayed(d):

                    @pl.when(even(zp))
                    def _():
                        for half in range(2):
                            dpcopy(zp, d, part, half).wait_send()


def shards(queries, keys, values, grad_out, out_weight):
    vmem = pl.BlockSpec(memory_space=pltpu.VMEM)
    hbm = pl.BlockSpec(memory_space=pltpu.HBM)
    dma = pltpu.SemaphoreType.DMA
    pairs = [
        (2, 12), (1,), (2,), (4, 2), (2, 3, 2), (8, 2),
        (3,), (3,), (4, 2), (5, 2, 2),
    ]
    sems = [dma((5,))]
    for shape in pairs:
        sems += [dma(shape), dma(shape)]
    sems += [dma((4, 2, 2)), dma((2, 3, 2)), dma((3,)), dma((3,))]
    block = pltpu.VMEM((SEQ, WIDTH), BF)
    operands = (queries, keys, values, grad_out, out_weight.reshape(2, HALF, WIDTH))
    operands = [pltpu.with_memory_space_constraint(a, pltpu.HBM) for a in operands]
    d_attention, d_weight = pl.pallas_call(
        kernel,
        out_shape=(
            jax.ShapeDtypeStruct((3, SEQ, WIDTH), BF),
            jax.ShapeDtypeStruct((2, HALF, WIDTH), F32),
        ),
        in_specs=[hbm] * 5,
        out_specs=(vmem,) * 2,
        scratch_shapes=[
            block,
            block,
            block,
            block,
            pltpu.VMEM((2, HALF, WIDTH), BF),
            pltpu.VMEM((2, HALF, SEQ), BF),
            pltpu.VMEM((8, 2, HALF, SEQ), BF),
            pltpu.VMEM((8, SEQ, WIDTH), BF),
            pltpu.VMEM((8, 2, 2, HALF, WIDTH), BF),
            pltpu.VMEM((2 * HEADS, SEQ, HEAD_DIM), BF),
            pltpu.VMEM((HEADS, SEQ, SEQ), F32),
            pltpu.VMEM((2, SEQ, WIDTH), F32),
            pltpu.VMEM((HEADS, SEQ, HEAD_DIM), BF),
            pltpu.VMEM((HEADS, SEQ, HEAD_DIM), BF),
            block,
            pltpu.VMEM((8, 2, 2, HALF, WIDTH), BF),
            pltpu.VMEM((4, 2, 2, HALF, WIDTH), BF),
            pltpu.VMEM((5, 2, 2, HALF // 2, WIDTH), BF),
            pltpu.VMEM((2, 3, 2, HALF, WIDTH), BF),
            pltpu.VMEM((3, HALF, WIDTH), BF),
            pltpu.VMEM((3, HALF, WIDTH), BF),
            pltpu.VMEM((HALF, WIDTH), F32),
        ]
        + sems,
        compiler_params=pltpu.CompilerParams(
            collective_id=1, has_side_effects=True, vmem_limit_bytes=44 << 20
        ),
        cost_estimate=pl.CostEstimate(
            flops=6_000_000_000, bytes_accessed=4_000_000, transcendentals=800_000
        ),
    )(*operands)
    return d_attention[0], d_attention[1], d_attention[2], d_weight.reshape(WIDTH, WIDTH)


def solution(mesh):
    placed = P("fsdp", "tensor")
    return jax.shard_map(
        shards,
        mesh=mesh,
        in_specs=(placed,) * 5,
        out_specs=(placed,) * 4,
        check_vma=False,
    )
```
